32 devices in a mesh: tile: 8 (over z, x), pos: 4 (over y, core).
Axes of the slice: x: 2, y: 2, z: 4, core: 2. Of those that a mesh axis runs over, the one named last changes fastest.
Arguments:
- obj_real: float32 [4, 2048, 256], P(None, ('tile', 'pos')), may hold values from 0.5 to 1.5
- obj_imag: float32 [4, 2048, 256], P(None, ('tile', 'pos')), may hold values from -4 to 4
- probe: float32 [2, 128, 128], replicated, may hold values from -6 to 6
- fresnel_phase: float32 [33], replicated, may hold values from -3.140625 to 3.140625
- row_offset: int32 [512], P('tile'), may hold values from 0 to 255
- col_offset: int32 [512], P('tile'), may hold values from 0 to 128
- live_count: int32 [8], P('tile'), may hold values from 16 to 64, as said below
- measured: bfloat16 [512, 128, 128], P('tile'), may hold values from 0.19921875 to 2
Outputs:
- grad_real: float32 [4, 2048, 256], P(None, ('tile', 'pos'))
- grad_imag: float32 [4, 2048, 256], P(None, ('tile', 'pos'))
The draws below stay inside these ranges and needn't reach their ends.
Inputs may be any that keep to these rules, and one draw needn't show every extreme that they name: `row_offset`: row offsets count from the first of the 256 rows of the position's band. Band g uses its first live_count[g] slots; some band uses all 64.
All inputs are finite; a program needn't handle non-finite values.
Results may differ from the reference program's by a relative error of at most 0.012.
The reference program's roundings to bfloat16 on the way (of `kernel` and `dft`) count: a program that leaves them out, or rounds other values in their place, can miss the bound.
Values sent between devices are 32-bit elements; how exact they have to be, the bound alone decides.
A program may use at most 64 MiB of HBM per device.

```python
import jax
import jax.numpy as jnp
from jax import lax

PATCH = 128
SLICES = 4
TAPS = 33
CAP = 64
NC = 256
GROUPS = 8
GROUP_ROWS = 256
NR = 2048
NPOS = 512


def draw_live_count(key, part):
    groups = NPOS // CAP
    counts = jax.random.randint(key, (groups,), CAP // 4, CAP + 1, dtype=jnp.int32)
    full_group = jax.random.randint(jax.random.fold_in(key, 1), (), 0, groups, dtype=jnp.int32)
    return jnp.where(jnp.arange(groups, dtype=jnp.int32) == full_group, CAP, counts).astype(jnp.int32)


def plant(drawn, rng, smallest, high):
    longest = drawn.shape.index(max(drawn.shape))
    spots = []
    for shift in (0, 1):
        where = [jax.random.randint(jax.random.fold_in(rng, axis), (), 0, length) for axis, length in enumerate(drawn.shape)]
        where[longest] = (where[longest] + shift) % drawn.shape[longest]
        spots.append(tuple(where))
    return drawn.at[spots[0]].set(smallest).at[spots[1]].set(high)


def level_of(key, shape, split, low, top_value):
    def one(dim, shards_of):
        heights = jax.random.uniform(jax.random.fold_in(jax.random.fold_in(key, 6), dim), (shards_of,), jnp.float32, low / len(split), top_value / len(split))
        return jnp.repeat(jnp.exp(heights), shape[dim] // shards_of).reshape((-1,) + (1,) * (len(shape) - dim - 1))

    factor_of = one(*split[0])
    for cut in split[1:]:
        factor_of = factor_of * one(*cut)
    return factor_of


def gaussian(own_key, shape, width, most, split=(), held_as=jnp.bfloat16):
    gain = level_of(own_key, shape, split, -0.22, 0.18) if split else 1.0
    array = jax.random.normal(own_key, shape, jnp.float32) * width * gain
    return jnp.minimum(jnp.maximum(array, -most), most).astype(held_as)


def setup_inputs(seed: int = 0) -> dict:
    splits = jax.random.split(jax.random.key(seed), 9)
    return {
        "obj_real": jnp.clip(1.0 + 0.1 * jax.random.normal(splits[0], (SLICES, NR, NC), jnp.float32), 0.5, 1.5),
        "obj_imag": gaussian(splits[1], (SLICES, NR, NC), 0.3, 4.0, ((1, 32),), jnp.float32),
        "probe": gaussian(splits[2], (2, PATCH, PATCH), 1.0, 6.0, (), jnp.float32),
        "fresnel_phase": jnp.clip(jax.random.uniform(splits[3], (TAPS,), jnp.float32, -3.140625, 3.140625), -3.140625, 3.140625),
        "row_offset": plant(jax.random.randint(splits[4], (NPOS,), 0, GROUP_ROWS), jax.random.fold_in(splits[4], 1), 0, GROUP_ROWS - 1).astype(jnp.int32),
        "col_offset": plant(jax.random.randint(splits[5], (NPOS,), 0, NC - PATCH + 1), jax.random.fold_in(splits[5], 1), 0, NC - PATCH).astype(jnp.int32),
        "live_count": draw_live_count(jax.random.fold_in(splits[8], 71), 0),
        "measured": jnp.clip(0.19921875 + 1.8007812 * jax.random.uniform(splits[7], (NPOS, PATCH, PATCH), jnp.float32) ** level_of(splits[7], (NPOS, PATCH, PATCH), ((0, 8),), -0.2, 0.2), 0.19921875, 2.0).astype(jnp.bfloat16),
    }


AMP_FLOOR = 0.25

def half_dot(left, right):
    return jnp.dot(left.astype(jnp.bfloat16), right.astype(jnp.bfloat16), preferred_element_type=jnp.float32)

def complex_dot(left, right):
    real = half_dot(left[0], right[0]) - half_dot(left[1], right[1])
    imag = half_dot(left[0], right[1]) + half_dot(left[1], right[0])
    return (real, imag)

def two_sided(matrix, wave):
    inner = complex_dot(matrix, wave)
    return complex_dot(inner, (matrix[0].T, matrix[1].T))

def tables(phase, patch):
    taps = phase.shape[0]
    rows = jnp.arange(patch, dtype=jnp.int32)[:, None]
    cols = jnp.arange(patch, dtype=jnp.int32)[None, :]
    offset = cols - rows + taps // 2
    picked = (offset[:, :, None] == jnp.arange(taps, dtype=jnp.int32)[None, None, :]).astype(phase.dtype)
    scale = 1.0 / jnp.sqrt(jnp.asarray(taps, phase.dtype))
    kern_re = (lax.optimization_barrier(jnp.sum(picked * jnp.cos(phase), axis=-1)) * scale).astype(jnp.bfloat16)
    kern_im = (lax.optimization_barrier(jnp.sum(picked * jnp.sin(phase), axis=-1)) * scale).astype(jnp.bfloat16)
    product = rows * cols % patch
    angle = 2.0 * jnp.pi / patch * product.astype(phase.dtype)
    norm = 1.0 / jnp.sqrt(jnp.asarray(patch, phase.dtype))
    dft_re = (jnp.cos(angle) * norm).astype(jnp.bfloat16)
    dft_im = (-jnp.sin(angle) * norm).astype(jnp.bfloat16)
    return ((kern_re, kern_im), (dft_re, dft_im))

def exit_loss(piece_re, piece_im, probe, target, weight, kernel, dft):
    wave_re, wave_im = (probe[0], probe[1])
    slices = piece_re.shape[0]
    for layer in range(slices):
        o_re, o_im = (piece_re[layer], piece_im[layer])
        wave_re, wave_im = (wave_re * o_re - wave_im * o_im, wave_re * o_im + wave_im * o_re)
        if layer + 1 < slices:
            wave_re, wave_im = two_sided(kernel, (wave_re, wave_im))
    far_re, far_im = two_sided(dft, (wave_re, wave_im))
    amplitude = jnp.sqrt(far_re * far_re + far_im * far_im + AMP_FLOOR)
    return 0.5 * weight * jnp.sum((amplitude - target) ** 2)

def reference(obj_real, obj_imag, probe, fresnel_phase, row_offset, col_offset, live_count, measured):
    kernel, dft = tables(fresnel_phase, PATCH)
    spare = jnp.zeros((SLICES, PATCH, NC), obj_real.dtype)
    ext_re = jnp.concatenate([obj_real, spare], axis=1)
    ext_im = jnp.concatenate([obj_imag, spare], axis=1)
    targets_all = measured.astype(jnp.float32)
    zero = jnp.zeros((), jnp.int32)
    grad_many = jax.vmap(jax.grad(exit_loss, argnums=(0, 1)), in_axes=(0, 0, None, 0, 0, None, None))

    def cut(field, top, left):
        return lax.dynamic_slice(field, (zero, top, left), (SLICES, PATCH, PATCH))

    def per_group(carry, group):
        first = group * CAP
        tops = group * GROUP_ROWS + lax.dynamic_slice_in_dim(row_offset, first, CAP)
        lefts = lax.dynamic_slice_in_dim(col_offset, first, CAP)
        targets = lax.dynamic_slice_in_dim(targets_all, first, CAP)
        live = lax.dynamic_index_in_dim(live_count, group, keepdims=False)
        weights = (jnp.arange(CAP, dtype=jnp.int32) < live).astype(obj_real.dtype)
        pieces_re = jax.vmap(cut, in_axes=(None, 0, 0))(ext_re, tops, lefts)
        pieces_im = jax.vmap(cut, in_axes=(None, 0, 0))(ext_im, tops, lefts)
        grads_re, grads_im = grad_many(pieces_re, pieces_im, probe, targets, weights, kernel, dft)

        def add_one(acc, item):
            top, left, one_re, one_im = item
            acc_re = lax.dynamic_update_slice(acc[0], cut(acc[0], top, left) + one_re, (zero, top, left))
            acc_im = lax.dynamic_update_slice(acc[1], cut(acc[1], top, left) + one_im, (zero, top, left))
            return ((acc_re, acc_im), None)
        carry, _ = lax.scan(add_one, carry, (tops, lefts, grads_re, grads_im))
        return (carry, None)
    start = (jnp.zeros_like(ext_re), jnp.zeros_like(ext_im))
    (acc_re, acc_im), _ = lax.scan(per_group, start, jnp.arange(GROUPS, dtype=jnp.int32))
    return (acc_re[:, :NR], acc_im[:, :NR])
```

```python
import functools

import jax
import jax.numpy as jnp
import ml_dtypes
import numpy as np
from jax import lax
from jax.experimental import pallas as pl
from jax.experimental.pallas import tpu as pltpu
from jax.sharding import PartitionSpec as P

AMP_FLOOR = 0.25
BATCH = 4


def dft_tables(patch):
    grid = np.arange(patch)
    product = (grid[:, None] * grid[None, :] % patch).astype(np.float32)
    angle = np.float32(2.0 * np.pi / patch) * product
    norm = np.float32(1.0) / np.sqrt(np.float32(patch))
    real = (np.cos(angle) * norm).astype(ml_dtypes.bfloat16)
    imag = (-np.sin(angle) * norm).astype(ml_dtypes.bfloat16)
    left = np.block([[real, -imag], [imag, real]])
    right = np.block([[real.T, imag.T], [-imag.T, real.T]])
    return jnp.asarray(left), jnp.asarray(right)


def dot(left, right):
    return jnp.dot(left, right, preferred_element_type=jnp.float32)


def stack_rows(pairs):
    return jnp.concatenate([jnp.concatenate(pair, axis=0) for pair in pairs], axis=1)


def stack_cols(pairs):
    return jnp.concatenate([jnp.concatenate(pair, axis=1) for pair in pairs], axis=0)


def split_rows(array, patch):
    count = array.shape[1] // patch
    return [
        (array[:patch, b * patch : (b + 1) * patch], array[patch:, b * patch : (b + 1) * patch])
        for b in range(count)
    ]


def split_cols(array, patch):
    count = array.shape[0] // patch
    return [
        (array[b * patch : (b + 1) * patch, :patch], array[b * patch : (b + 1) * patch, patch:])
        for b in range(count)
    ]


def halves(pairs):
    return [(a.astype(jnp.bfloat16), b.astype(jnp.bfloat16)) for a, b in pairs]


def forward_two_sided(left, right, pairs):
    patch = pairs[0][0].shape[0]
    inner = split_rows(dot(left, stack_rows(halves(pairs))), patch)
    return split_cols(dot(stack_cols(halves(inner)), right), patch)


def backward_two_sided(left, right, pairs):
    patch = pairs[0][0].shape[0]
    inner = split_cols(dot(stack_cols(halves(pairs)), left), patch)
    return split_rows(dot(right, stack_rows(halves(inner))), patch)


def compute_kernel(
    taps, rows_ref, cols_ref, live_ref, phase_ref, dft_left, dft_right, probe_ref,
    own_re, own_im, sib_re, sib_im, far_re, far_im, farsib_re, farsib_im, measured_ref,
    keep_ref, give_ref, spill_ref, spillgive_ref,
    window, acc, target, kern_left, kern_right, saved, patches, listed, in_sem, target_sem, out_sem,
):
    slices, shard, width = own_re.shape
    patch = probe_ref.shape[-1]
    slots = rows_ref.shape[0]
    parts = width // patch
    member = lax.axis_index("pos")
    pair, parity = member // 2, member % 2
    get_target = pltpu.make_async_copy(measured_ref, target, target_sem)
    get_target.start()
    loads = []
    sources = ((own_re, own_im), (sib_re, sib_im), (far_re, far_im), (farsib_re, farsib_im))
    spots = (parity, 1 - parity, 2 + parity, 3 - parity)
    for source, spot in zip(sources, spots):
        for part in range(2):
            for half in range(parts):
                loads.append(
                    pltpu.make_async_copy(
                        source[part].at[:, :, pl.ds(half * patch, patch)],
                        window.at[part, :, half, pl.ds(spot * shard, shard), :],
                        in_sem.at[len(loads)],
                    )
                )
    for load in loads:
        load.start()

    def pick(slot, count):
        ok = jnp.logical_and(slot < live_ref[0], rows_ref[slot] // (2 * shard) == pair)
        take = jnp.logical_and(ok, count % 2 == parity)
        listed[jnp.where(take, count // 2, slots)] = slot
        return count + ok.astype(jnp.int32)

    total = lax.fori_loop(0, slots, pick, jnp.int32(0))
    mine = (total + 1 - parity) // 2

    row = lax.broadcasted_iota(jnp.int32, (patch, patch), 0)
    col = lax.broadcasted_iota(jnp.int32, (patch, patch), 1)
    band = jnp.logical_and(col - row + taps // 2 >= 0, col - row + taps // 2 < taps)
    scale = 1.0 / jnp.sqrt(jnp.float32(taps))

    def toeplitz(values):
        wide = jnp.broadcast_to(values, (patch, patch))
        moved = pltpu.roll(wide, patch - taps // 2, 1, stride=1, stride_axis=0)
        return jnp.where(band, moved, 0.0)

    kern_re = toeplitz(jnp.cos(phase_ref[...]) * scale)
    kern_im = toeplitz(jnp.sin(phase_ref[...]) * scale)
    kern_left[...] = stack_rows(halves([(kern_re, kern_im), (-kern_im, kern_re)]))
    kern_re_t, kern_im_t = kern_re.T, kern_im.T
    kern_right[...] = stack_rows(halves([(kern_re_t, -kern_im_t), (kern_im_t, kern_re_t)]))
    acc[...] = jnp.zeros_like(acc)
    for load in loads:
        load.wait()
    get_target.wait()

    def group(step, carry):
        first = step * BATCH
        index = [listed[jnp.minimum(first + b, mine - 1)] for b in range(BATCH)]
        weight = [(first + b < mine).astype(jnp.float32) for b in range(BATCH)]
        top = [rows_ref[i] - pair * (2 * shard) for i in index]
        left = [cols_ref[i] for i in index]
        back = [(patch - x) % patch for x in left]
        forth = [x % patch for x in left]
        inside = [col >= x for x in left]

        def cut(layer, b, part):
            a0 = window[part, layer, 0, pl.ds(top[b], patch), :]
            a1 = window[part, layer, 1, pl.ds(top[b], patch), :]
            return pltpu.roll(jnp.where(inside[b], a0, a1), back[b], 1)

        waves = [(probe_ref[0], probe_ref[1]) for _ in range(BATCH)]
        for layer in range(slices):
            nxt = []
            for b in range(BATCH):
                o_re, o_im = cut(layer, b, 0), cut(layer, b, 1)
                w_re, w_im = waves[b]
                if layer:
                    patches[layer - 1, b, 0] = o_re
                    patches[layer - 1, b, 1] = o_im
                    saved[layer - 1, b, 0] = w_re
                    saved[layer - 1, b, 1] = w_im
                nxt.append((w_re * o_re - w_im * o_im, w_re * o_im + w_im * o_re))
            if layer + 1 < slices:
                waves = forward_two_sided(kern_left[...], kern_right[...], nxt)
            else:
                waves = forward_two_sided(dft_left[...], dft_right[...], nxt)
        grads = []
        for b in range(BATCH):
            f_re, f_im = waves[b]
            amplitude = jnp.sqrt(f_re * f_re + f_im * f_im + AMP_FLOOR)
            t = target[index[b]].astype(jnp.float32)
            ratio = weight[b] * (amplitude - t) / amplitude
            grads.append((f_re * ratio, f_im * ratio))
        grads = backward_two_sided(dft_left[...], dft_right[...], grads)
        for layer in reversed(range(slices)):
            nxt = []
            for b in range(BATCH):
                g_re, g_im = grads[b]
                if layer:
                    w_re, w_im = saved[layer - 1, b, 0], saved[layer - 1, b, 1]
                    o_re, o_im = patches[layer - 1, b, 0], patches[layer - 1, b, 1]
                    nxt.append((o_re * g_re + o_im * g_im, o_re * g_im - o_im * g_re))
                else:
                    w_re, w_im = probe_ref[0], probe_ref[1]
                terms = (w_re * g_re + w_im * g_im, w_re * g_im - w_im * g_re)
                for part in range(2):
                    moved = pltpu.roll(terms[part], forth[b], 1)
                    spot = pl.ds(top[b], patch)
                    acc[part, layer, 0, spot, :] += jnp.where(inside[b], moved, 0.0)
                    acc[part, layer, 1, spot, :] += jnp.where(inside[b], 0.0, moved)
            if layer:
                grads = backward_two_sided(kern_left[...], kern_right[...], nxt)
        return carry

    lax.fori_loop(0, (mine + BATCH - 1) // BATCH, group, 0)

    stores = []
    for result, spot in zip((keep_ref, give_ref, spill_ref, spillgive_ref), spots):
        for part in range(2):
            for half in range(parts):
                stores.append(
                    pltpu.make_async_copy(
                        acc.at[part, :, half, pl.ds(spot * shard, shard), :],
                        result.at[part, :, :, pl.ds(half * patch, patch)],
                        out_sem.at[len(stores)],
                    )
                )
    for store in stores:
        store.start()
    for store in stores:
        store.wait()


def local(obj_real, obj_imag, probe, fresnel_phase, row_offset, col_offset, live_count, measured):
    slices, shard, width = obj_real.shape
    patch = probe.shape[-1]
    members = lax.axis_size("pos")
    devices = lax.axis_size("tile") * members
    parts = width // patch
    taps = fresnel_phase.shape[0]
    both = ("tile", "pos")
    swap = [(d, d ^ 1) for d in range(members)]
    sib_re, sib_im = lax.ppermute((obj_real, obj_imag), "pos", swap)
    up = [(d, d - 2) for d in range(2, devices)]
    far_re, far_im = lax.ppermute((obj_real, obj_imag), both, up)
    farsib_re, farsib_im = lax.ppermute((far_re, far_im), "pos", swap)
    phase = jnp.pad(fresnel_phase, (0, patch - taps)).reshape(1, patch)
    dft_left, dft_right = dft_tables(patch)
    block = jax.ShapeDtypeStruct((2, slices, shard, width), jnp.float32)
    smem = pl.BlockSpec(memory_space=pltpu.SMEM)
    vmem = pl.BlockSpec(memory_space=pltpu.VMEM)
    anywhere = pl.BlockSpec(memory_space=pl.ANY)
    keep, give, spill, spillgive = pl.pallas_call(
        functools.partial(compute_kernel, taps),
        out_shape=[block] * 4,
        in_specs=[smem] * 3 + [vmem] * 4 + [anywhere] * 9,
        out_specs=[anywhere] * 4,
        scratch_shapes=[
            pltpu.VMEM((2, slices, parts, 4 * shard, patch), jnp.float32),
            pltpu.VMEM((2, slices, parts, 4 * shard, patch), jnp.float32),
            pltpu.VMEM(measured.shape, measured.dtype),
            pltpu.VMEM((2 * patch, 2 * patch), jnp.bfloat16),
            pltpu.VMEM((2 * patch, 2 * patch), jnp.bfloat16),
            pltpu.VMEM((slices - 1, BATCH, 2, patch, patch), jnp.float32),
            pltpu.VMEM((slices - 1, BATCH, 2, patch, patch), jnp.float32),
            pltpu.SMEM((row_offset.shape[0] + 8,), jnp.int32),
            pltpu.SemaphoreType.DMA((8 * parts,)),
            pltpu.SemaphoreType.DMA,
            pltpu.SemaphoreType.DMA((8 * parts,)),
        ],
        compiler_params=pltpu.CompilerParams(vmem_limit_bytes=40 * 1024 * 1024),
    )(
        row_offset, col_offset, live_count, phase, dft_left, dft_right, probe,
        obj_real, obj_imag, sib_re, sib_im, far_re, far_im, farsib_re, farsib_im, measured,
    )
    sib, spillsib = lax.ppermute((give, spillgive), "pos", swap)
    down = [(d, d + 2) for d in range(devices - 2)]
    behind = lax.ppermute(spill + spillsib, both, down)
    total = keep + sib + behind
    return total[0], total[1]


def solution(mesh):
    in_specs = (
        P(None, ("tile", "pos"), None),
        P(None, ("tile", "pos"), None),
        P(),
        P(),
        P("tile"),
        P("tile"),
        P("tile"),
        P("tile", None, None),
    )
    out_specs = (P(None, ("tile", "pos"), None), P(None, ("tile", "pos"), None))
    return jax.shard_map(local, mesh=mesh, in_specs=in_specs, out_specs=out_specs, check_vma=False)
```

```python
import functools

import jax
import jax.numpy as jnp
import ml_dtypes
import numpy as np
from jax import lax
from jax.experimental import pallas as pl
from jax.experimental.pallas import tpu as pltpu
from jax.sharding import PartitionSpec as P

AMP_FLOOR = 0.25
BATCH = 4
VMEM_BYTES = 60 * 1024 * 1024


def dft_tables(patch):
    grid = np.arange(patch)
    product = (grid[:, None] * grid[None, :] % patch).astype(np.float32)
    angle = np.float32(2.0 * np.pi / patch) * product
    norm = np.float32(1.0) / np.sqrt(np.float32(patch))
    real = (np.cos(angle) * norm).astype(ml_dtypes.bfloat16)
    imag = (-np.sin(angle) * norm).astype(ml_dtypes.bfloat16)
    left = np.block([[real, -imag], [imag, real]])
    right = np.block([[real.T, imag.T], [-imag.T, real.T]])
    return jnp.asarray(left), jnp.asarray(right)


def dot(left, right):
    return jnp.dot(left, right, preferred_element_type=jnp.float32)


def stack_rows(pairs):
    return jnp.concatenate([jnp.concatenate(pair, axis=0) for pair in pairs], axis=1)


def stack_cols(pairs):
    return jnp.concatenate([jnp.concatenate(pair, axis=1) for pair in pairs], axis=0)


def split_rows(array, patch):
    count = array.shape[1] // patch
    return [
        (array[:patch, b * patch : (b + 1) * patch], array[patch:, b * patch : (b + 1) * patch])
        for b in range(count)
    ]


def split_cols(array, patch):
    count = array.shape[0] // patch
    return [
        (array[b * patch : (b + 1) * patch, :patch], array[b * patch : (b + 1) * patch, patch:])
        for b in range(count)
    ]


def halves(pairs):
    return [(a.astype(jnp.bfloat16), b.astype(jnp.bfloat16)) for a, b in pairs]


def forward_two_sided(left, right, pairs):
    patch = pairs[0][0].shape[0]
    inner = split_rows(dot(left, stack_rows(halves(pairs))), patch)
    return split_cols(dot(stack_cols(halves(inner)), right), patch)


def backward_two_sided(left, right, pairs):
    patch = pairs[0][0].shape[0]
    inner = split_cols(dot(stack_cols(halves(pairs)), left), patch)
    return split_rows(dot(right, stack_rows(halves(inner))), patch)


def compute_kernel(
    taps, rows_ref, cols_ref, live_ref, phase_ref, dft_left, dft_right, probe_ref,
    own_re, own_im, sib_ref, far_ref, farsib_ref, measured_ref,
    keep_ref, give_ref, spill_ref, spillgive_ref,
    window, acc, target, kern_left, kern_right, saved, patches, listed, in_sem, target_sem, out_sem,
):
    slices, shard, width = own_re.shape
    patch = probe_ref.shape[-1]
    slots = rows_ref.shape[0]
    parts = width // patch
    member = lax.axis_index("pos")
    pair, parity = member // 2, member % 2
    get_target = pltpu.make_async_copy(measured_ref, target, target_sem)
    get_target.start()
    has_up = lax.axis_index("tile") * lax.axis_size("pos") + member < lax.axis_size(
        "tile"
    ) * lax.axis_size("pos") - 2
    loads = []
    sources = (
        (own_re, own_im),
        (sib_ref.at[0], sib_ref.at[1]),
        (far_ref.at[0], far_ref.at[1]),
        (farsib_ref.at[0], farsib_ref.at[1]),
    )
    spots = (parity, 1 - parity, 2 + parity, 3 - parity)
    for source, spot in zip(sources, spots):
        for part in range(2):
            for half in range(parts):
                loads.append(
                    pltpu.make_async_copy(
                        source[part].at[:, :, pl.ds(half * patch, patch)],
                        window.at[part, :, half, pl.ds(spot * shard, shard), :],
                        in_sem.at[len(loads)],
                    )
                )
    inner_loads, far_loads = loads[: 4 * parts], loads[4 * parts :]
    for load in inner_loads:
        load.start()

    @pl.when(has_up)
    def _():
        for load in far_loads:
            load.start()

    @pl.when(jnp.logical_not(has_up))
    def _():
        window[:, :, :, 2 * shard :, :] = jnp.zeros(
            window.shape[:3] + (2 * shard, patch), window.dtype
        )

    def pick(slot, count):
        ok = jnp.logical_and(slot < live_ref[0], rows_ref[slot] // (2 * shard) == pair)
        take = jnp.logical_and(ok, count % 2 == parity)
        listed[jnp.where(take, count // 2, slots)] = slot
        return count + ok.astype(jnp.int32)

    total = lax.fori_loop(0, slots, pick, jnp.int32(0))
    mine = (total + 1 - parity) // 2

    row = lax.broadcasted_iota(jnp.int32, (patch, patch), 0)
    col = lax.broadcasted_iota(jnp.int32, (patch, patch), 1)
    band = jnp.logical_and(col - row + taps // 2 >= 0, col - row + taps // 2 < taps)
    scale = 1.0 / jnp.sqrt(jnp.float32(taps))

    def toeplitz(values):
        wide = jnp.broadcast_to(values, (patch, patch))
        moved = pltpu.roll(wide, patch - taps // 2, 1, stride=1, stride_axis=0)
        return jnp.where(band, moved, 0.0)

    kern_re = toeplitz(jnp.cos(phase_ref[...]) * scale)
    kern_im = toeplitz(jnp.sin(phase_ref[...]) * scale)
    kern_left[...] = stack_rows(halves([(kern_re, kern_im), (-kern_im, kern_re)]))
    kern_re_t, kern_im_t = kern_re.T, kern_im.T
    kern_right[...] = stack_rows(halves([(kern_re_t, -kern_im_t), (kern_im_t, kern_re_t)]))
    acc[...] = jnp.zeros_like(acc)
    for load in inner_loads:
        load.wait()

    @pl.when(has_up)
    def _():
        for load in far_loads:
            load.wait()

    get_target.wait()

    def group(step, carry):
        first = step * BATCH
        index = [listed[jnp.minimum(first + b, mine - 1)] for b in range(BATCH)]
        weight = [(first + b < mine).astype(jnp.float32) for b in range(BATCH)]
        top = [rows_ref[i] - pair * (2 * shard) for i in index]
        left = [cols_ref[i] for i in index]
        back = [(patch - x) % patch for x in left]
        forth = [x % patch for x in left]
        inside = [col >= x for x in left]

        def cut(layer, b, part):
            a0 = window[part, layer, 0, pl.ds(top[b], patch), :]
            a1 = window[part, layer, 1, pl.ds(top[b], patch), :]
            return pltpu.roll(jnp.where(inside[b], a0, a1), back[b], 1)

        waves = [(probe_ref[0], probe_ref[1]) for _ in range(BATCH)]
        for layer in range(slices):
            nxt = []
            for b in range(BATCH):
                o_re, o_im = cut(layer, b, 0), cut(layer, b, 1)
                w_re, w_im = waves[b]
                if layer:
                    patches[layer - 1, b, 0] = o_re
                    patches[layer - 1, b, 1] = o_im
                    saved[layer - 1, b, 0] = w_re
                    saved[layer - 1, b, 1] = w_im
                nxt.append((w_re * o_re - w_im * o_im, w_re * o_im + w_im * o_re))
            if layer + 1 < slices:
                waves = forward_two_sided(kern_left[...], kern_right[...], nxt)
            else:
                waves = forward_two_sided(dft_left[...], dft_right[...], nxt)
        grads = []
        for b in range(BATCH):
            f_re, f_im = waves[b]
            amplitude = jnp.sqrt(f_re * f_re + f_im * f_im + AMP_FLOOR)
            t = target[index[b]].astype(jnp.float32)
            ratio = weight[b] * (amplitude - t) / amplitude
            grads.append((f_re * ratio, f_im * ratio))
        grads = backward_two_sided(dft_left[...], dft_right[...], grads)
        for layer in reversed(range(slices)):
            nxt = []
            for b in range(BATCH):
                g_re, g_im = grads[b]
                if layer:
                    w_re, w_im = saved[layer - 1, b, 0], saved[layer - 1, b, 1]
                    o_re, o_im = patches[layer - 1, b, 0], patches[layer - 1, b, 1]
                    nxt.append((o_re * g_re + o_im * g_im, o_re * g_im - o_im * g_re))
                else:
                    w_re, w_im = probe_ref[0], probe_ref[1]
                terms = (w_re * g_re + w_im * g_im, w_re * g_im - w_im * g_re)
                for part in range(2):
                    moved = pltpu.roll(terms[part], forth[b], 1)
                    spot = pl.ds(top[b], patch)
                    acc[part, layer, 0, spot, :] += jnp.where(inside[b], moved, 0.0)
                    acc[part, layer, 1, spot, :] += jnp.where(inside[b], 0.0, moved)
            if layer:
                grads = backward_two_sided(kern_left[...], kern_right[...], nxt)
        return carry

    lax.fori_loop(0, (mine + BATCH - 1) // BATCH, group, 0)

    stores = []
    for result, spot in zip((keep_ref, give_ref, spill_ref, spillgive_ref), spots):
        for part in range(2):
            for half in range(parts):
                stores.append(
                    pltpu.make_async_copy(
                        acc.at[part, :, half, pl.ds(spot * shard, shard), :],
                        result.at[part, :, :, pl.ds(half * patch, patch)],
                        out_sem.at[len(stores)],
                    )
                )
    for store in stores:
        store.start()
    for store in stores:
        store.wait()


def neighbours():
    tile, pos = lax.axis_index("tile"), lax.axis_index("pos")
    members = lax.axis_size("pos")
    devices = lax.axis_size("tile") * members
    me = tile * members + pos
    below, above = (me + devices - 2) % devices, (me + 2) % devices
    sibling = (tile, pos + 1 - 2 * (pos % 2))
    lower, upper = (below // members, below % members), (above // members, above % members)
    return sibling, lower, upper, me >= 2, me < devices - 2


def greet(sibling, lower, upper, has_down, has_up):
    barrier = pltpu.get_barrier_semaphore()
    mesh_ids = pl.DeviceIdType.MESH
    pl.semaphore_signal(barrier, inc=1, device_id=sibling, device_id_type=mesh_ids)

    @pl.when(has_down)
    def _():
        pl.semaphore_signal(barrier, inc=1, device_id=lower, device_id_type=mesh_ids)

    @pl.when(has_up)
    def _():
        pl.semaphore_signal(barrier, inc=1, device_id=upper, device_id_type=mesh_ids)

    pl.semaphore_wait(barrier, 1 + has_down.astype(jnp.int32) + has_up.astype(jnp.int32))


def remote(source, target, send, receive, device):
    return pltpu.make_async_remote_copy(
        src_ref=source, dst_ref=target, send_sem=send, recv_sem=receive,
        device_id=device, device_id_type=pl.DeviceIdType.MESH,
    )


def gather_kernel(re_ref, im_ref, sib, far, farsib, far_send, far_recv, fwd_send, fwd_recv, sib_send, sib_recv):
    sibling, lower, upper, has_down, has_up = neighbours()
    slices = re_ref.shape[0]
    fields = (re_ref, im_ref)
    chunks = [(part, layer) for layer in range(slices) for part in range(2)]
    outward = [
        remote(fields[p].at[s], far.at[p, s], far_send.at[k], far_recv.at[k], lower)
        for k, (p, s) in enumerate(chunks)
    ]
    onward = [
        remote(far.at[p, s], farsib.at[p, s], fwd_send.at[k], fwd_recv.at[k], sibling)
        for k, (p, s) in enumerate(chunks)
    ]
    across = [remote(fields[p], sib.at[p], sib_send.at[p], sib_recv.at[p], sibling) for p in range(2)]
    greet(sibling, lower, upper, has_down, has_up)

    @pl.when(has_down)
    def _():
        for copy in outward:
            copy.start()

    for copy in across:
        copy.start()

    @pl.when(has_up)
    def _():
        for come, go in zip(outward, onward):
            come.wait_recv()
            go.start()
        for go in onward:
            go.wait()

    for copy in across:
        copy.wait()

    @pl.when(has_down)
    def _():
        for copy in outward:
            copy.wait_send()


def scatter_kernel(
    keep, give, spill, spillgive, out_re, out_im,
    kept, spilled, given, crossed, total, behind,
    load_sem, keep_sem, cross_send, cross_recv, give_send, give_recv, up_send, up_recv,
):
    sibling, lower, upper, has_down, has_up = neighbours()
    slices = out_re.shape[0]
    outs = (out_re, out_im)
    chunks = [(part, layer) for layer in range(slices) for part in range(2)]
    across = [
        remote(spillgive.at[p, s], crossed.at[p, s], cross_send.at[k], cross_recv.at[k], sibling)
        for k, (p, s) in enumerate(chunks)
    ]
    gifts = [remote(give.at[p], given.at[p], give_send.at[p], give_recv.at[p], sibling) for p in range(2)]
    upward = [
        remote(total.at[p, s], behind.at[p, s], up_send.at[k], up_recv.at[k], upper)
        for k, (p, s) in enumerate(chunks)
    ]
    loads = [
        pltpu.make_async_copy(spill.at[p, s], spilled.at[p, s], load_sem.at[k])
        for k, (p, s) in enumerate(chunks)
    ]
    load_keep = pltpu.make_async_copy(keep, kept, keep_sem)
    for load in loads:
        load.start()
    greet(sibling, lower, upper, has_down, has_up)
    for copy in across:
        copy.start()
    for copy in gifts:
        copy.start()
    load_keep.start()
    for k, (p, s) in enumerate(chunks):
        loads[k].wait()
        across[k].wait_recv()
        total[p, s] = spilled[p, s] + crossed[p, s]

        @pl.when(has_up)
        def _():
            upward[k].start()

    load_keep.wait()
    for copy in gifts:
        copy.wait()
    for p in range(2):
        outs[p][...] = kept[p] + given[p]

    @pl.when(has_down)
    def _():
        for k, (p, s) in enumerate(chunks):
            upward[k].wait_recv()
            outs[p][s] = outs[p][s] + behind[p, s]

    for copy in across:
        copy.wait_send()

    @pl.when(has_up)
    def _():
        for copy in upward:
            copy.wait_send()


def local(obj_real, obj_imag, probe, fresnel_phase, row_offset, col_offset, live_count, measured):
    slices, shard, width = obj_real.shape
    patch = probe.shape[-1]
    parts = width // patch
    taps = fresnel_phase.shape[0]
    chunks = 2 * slices
    block = jax.ShapeDtypeStruct((2, slices, shard, width), jnp.float32)
    smem = pl.BlockSpec(memory_space=pltpu.SMEM)
    vmem = pl.BlockSpec(memory_space=pltpu.VMEM)
    anywhere = pl.BlockSpec(memory_space=pl.ANY)
    dma = pltpu.SemaphoreType.DMA
    sib, far, farsib = pl.pallas_call(
        gather_kernel,
        out_shape=[block] * 3,
        in_specs=[anywhere] * 2,
        out_specs=[anywhere] * 3,
        scratch_shapes=[dma((chunks,))] * 4 + [dma((2,))] * 2,
        compiler_params=pltpu.CompilerParams(
            collective_id=0, has_side_effects=True, vmem_limit_bytes=VMEM_BYTES
        ),
        name="gather_rows",
    )(obj_real, obj_imag)
    phase = jnp.pad(fresnel_phase, (0, patch - taps)).reshape(1, patch)
    dft_left, dft_right = dft_tables(patch)
    keep, give, spill, spillgive = pl.pallas_call(
        functools.partial(compute_kernel, taps),
        out_shape=[block] * 4,
        in_specs=[smem] * 3 + [vmem] * 4 + [anywhere] * 6,
        out_specs=[anywhere] * 4,
        scratch_shapes=[
            pltpu.VMEM((2, slices, parts, 4 * shard, patch), jnp.float32),
            pltpu.VMEM((2, slices, parts, 4 * shard, patch), jnp.float32),
            pltpu.VMEM(measured.shape, measured.dtype),
            pltpu.VMEM((2 * patch, 2 * patch), jnp.bfloat16),
            pltpu.VMEM((2 * patch, 2 * patch), jnp.bfloat16),
            pltpu.VMEM((slices - 1, BATCH, 2, patch, patch), jnp.float32),
            pltpu.VMEM((slices - 1, BATCH, 2, patch, patch), jnp.float32),
            pltpu.SMEM((row_offset.shape[0] + 8,), jnp.int32),
            pltpu.SemaphoreType.DMA((8 * parts,)),
            pltpu.SemaphoreType.DMA,
            pltpu.SemaphoreType.DMA((8 * parts,)),
        ],
        compiler_params=pltpu.CompilerParams(vmem_limit_bytes=VMEM_BYTES),
        name="patch_gradients",
    )(
        row_offset, col_offset, live_count, phase, dft_left, dft_right, probe,
        obj_real, obj_imag, sib, far, farsib, measured,
    )
    out = jax.ShapeDtypeStruct(obj_real.shape, jnp.float32)
    return tuple(
        pl.pallas_call(
            scatter_kernel,
            out_shape=[out] * 2,
            in_specs=[anywhere] * 4,
            out_specs=[vmem] * 2,
            scratch_shapes=[pltpu.VMEM(block.shape, jnp.float32)] * 6
            + [dma((chunks,)), dma]
            + [dma((chunks,))] * 2
            + [dma((2,))] * 2
            + [dma((chunks,))] * 2,
            compiler_params=pltpu.CompilerParams(
                collective_id=1, has_side_effects=True, vmem_limit_bytes=VMEM_BYTES
            ),
            name="scatter_rows",
        )(keep, give, spill, spillgive)
    )


def solution(mesh):
    in_specs = (
        P(None, ("tile", "pos"), None),
        P(None, ("tile", "pos"), None),
        P(),
        P(),
        P("tile"),
        P("tile"),
        P("tile"),
        P("tile", None, None),
    )
    out_specs = (P(None, ("tile", "pos"), None), P(None, ("tile", "pos"), None))
    return jax.shard_map(local, mesh=mesh, in_specs=in_specs, out_specs=out_specs, check_vma=False)
```

```python
import functools

import jax
import jax.numpy as jnp
import ml_dtypes
import numpy as np
from jax import lax
from jax.experimental import pallas as pl
from jax.experimental.pallas import tpu as pltpu
from jax.sharding import PartitionSpec as P

AMP_FLOOR = 0.25
BATCH = 4
CHAIN = 2
VMEM_BYTES = 60 * 1024 * 1024


def dft_tables(patch):
    grid = np.arange(patch)
    product = (grid[:, None] * grid[None, :] % patch).astype(np.float32)
    angle = np.float32(2.0 * np.pi / patch) * product
    norm = np.float32(1.0) / np.sqrt(np.float32(patch))
    real = (np.cos(angle) * norm).astype(ml_dtypes.bfloat16)
    imag = (-np.sin(angle) * norm).astype(ml_dtypes.bfloat16)
    left = np.block([[real, -imag], [imag, real]])
    right = np.block([[real.T, imag.T], [-imag.T, real.T]])
    return jnp.asarray(left), jnp.asarray(right)


def dot(left, right):
    return jnp.dot(left, right, preferred_element_type=jnp.float32)


def stack_rows(pairs):
    return jnp.concatenate([jnp.concatenate(pair, axis=0) for pair in pairs], axis=1)


def stack_cols(pairs):
    return jnp.concatenate([jnp.concatenate(pair, axis=1) for pair in pairs], axis=0)


def split_rows(array, patch):
    count = array.shape[1] // patch
    return [
        (array[:patch, b * patch : (b + 1) * patch], array[patch:, b * patch : (b + 1) * patch])
        for b in range(count)
    ]


def split_cols(array, patch):
    count = array.shape[0] // patch
    return [
        (array[b * patch : (b + 1) * patch, :patch], array[b * patch : (b + 1) * patch, patch:])
        for b in range(count)
    ]


def halves(pairs):
    return [(a.astype(jnp.bfloat16), b.astype(jnp.bfloat16)) for a, b in pairs]


def forward_two_sided(left, right, pairs):
    patch = pairs[0][0].shape[0]
    inner = split_rows(dot(left, stack_rows(halves(pairs))), patch)
    return split_cols(dot(stack_cols(halves(inner)), right), patch)


def backward_two_sided(left, right, pairs):
    patch = pairs[0][0].shape[0]
    inner = split_cols(dot(stack_cols(halves(pairs)), left), patch)
    return split_rows(dot(right, stack_rows(halves(inner))), patch)


def compute_kernel(
    taps, rows_ref, cols_ref, live_ref, phase_ref, dft_left, dft_right, probe_ref,
    own_re, own_im, near_ref, nearsib_ref, far_ref, farsib_ref, measured_ref,
    near_keep, near_give, far_keep, far_give,
    window, acc, target, kern_left, kern_right, saved, patches, listed, in_sem, target_sem, out_sem,
):
    slices, shard, width = own_re.shape
    patch = probe_ref.shape[-1]
    slots = rows_ref.shape[0]
    parts = width // patch
    member = lax.axis_index("pos")
    parity = member % 2
    get_target = pltpu.make_async_copy(measured_ref, target, target_sem)
    get_target.start()
    outer = member < 2
    ahead = jnp.logical_and(outer, lax.axis_index("tile") + 1 < lax.axis_size("tile"))
    base = jnp.where(outer, 2 * shard, 0)
    spots = (parity, 1 - parity, 2 + parity, 3 - parity)

    def loads_of(real, imag, place):
        return [
            pltpu.make_async_copy(
                source.at[:, :, pl.ds(half * patch, patch)],
                window.at[part, :, half, pl.ds(spots[place] * shard, shard), :],
                in_sem.at[(place * 2 + part) * parts + half],
            )
            for part, source in enumerate((real, imag))
            for half in range(parts)
        ]

    near_loads = loads_of(near_ref.at[0], near_ref.at[1], 0)
    near_loads += loads_of(nearsib_ref.at[0], nearsib_ref.at[1], 1)
    own_loads = loads_of(own_re, own_im, 2)
    far_loads = loads_of(far_ref.at[0], far_ref.at[1], 2)
    farsib_loads = loads_of(farsib_ref.at[0], farsib_ref.at[1], 3)
    for load in near_loads:
        load.start()

    @pl.when(jnp.logical_not(outer))
    def _():
        for load in own_loads + farsib_loads:
            load.start()

    @pl.when(ahead)
    def _():
        for load in far_loads + farsib_loads:
            load.start()

    @pl.when(jnp.logical_and(outer, jnp.logical_not(ahead)))
    def _():
        window[:, :, :, 2 * shard :, :] = jnp.zeros(
            window.shape[:3] + (2 * shard, patch), window.dtype
        )

    def pick(slot, count):
        ok = jnp.logical_and(slot < live_ref[0], (rows_ref[slot] >= 2 * shard) == outer)
        take = jnp.logical_and(ok, count % 2 == parity)
        listed[jnp.where(take, count // 2, slots)] = slot
        return count + ok.astype(jnp.int32)

    total = lax.fori_loop(0, slots, pick, jnp.int32(0))
    mine = (total + 1 - parity) // 2

    row = lax.broadcasted_iota(jnp.int32, (patch, patch), 0)
    col = lax.broadcasted_iota(jnp.int32, (patch, patch), 1)
    band = jnp.logical_and(col - row + taps // 2 >= 0, col - row + taps // 2 < taps)
    scale = 1.0 / jnp.sqrt(jnp.float32(taps))

    def toeplitz(values):
        wide = jnp.broadcast_to(values, (patch, patch))
        moved = pltpu.roll(wide, patch - taps // 2, 1, stride=1, stride_axis=0)
        return jnp.where(band, moved, 0.0)

    kern_re = toeplitz(jnp.cos(phase_ref[...]) * scale)
    kern_im = toeplitz(jnp.sin(phase_ref[...]) * scale)
    kern_left[...] = stack_rows(halves([(kern_re, kern_im), (-kern_im, kern_re)]))
    kern_re_t, kern_im_t = kern_re.T, kern_im.T
    kern_right[...] = stack_rows(halves([(kern_re_t, -kern_im_t), (kern_im_t, kern_re_t)]))
    acc[...] = jnp.zeros_like(acc)
    for load in near_loads:
        load.wait()

    @pl.when(jnp.logical_or(jnp.logical_not(outer), ahead))
    def _():
        for load in far_loads + farsib_loads:
            load.wait()

    get_target.wait()

    def group(first, size):
        every = range(size)
        chains = [list(every)[c : c + CHAIN] for c in range(0, size, CHAIN)]
        index = [listed[jnp.minimum(first + b, mine - 1)] for b in every]
        weight = [(first + b < mine).astype(jnp.float32) for b in every]
        top = [rows_ref[i] - base for i in index]
        left = [cols_ref[i] for i in index]
        back = [(patch - x) % patch for x in left]
        forth = [x % patch for x in left]
        inside = [col >= x for x in left]

        def cut(layer, b, part):
            a0 = window[part, layer, 0, pl.ds(top[b], patch), :]
            a1 = window[part, layer, 1, pl.ds(top[b], patch), :]
            return pltpu.roll(jnp.where(inside[b], a0, a1), back[b], 1)

        waves = [(probe_ref[0], probe_ref[1]) for _ in every]
        for layer in range(slices):
            for chain in chains:
                nxt = []
                for b in chain:
                    o_re, o_im = cut(layer, b, 0), cut(layer, b, 1)
                    w_re, w_im = waves[b]
                    if layer:
                        patches[layer - 1, b, 0] = o_re
                        patches[layer - 1, b, 1] = o_im
                        saved[layer - 1, b, 0] = w_re
                        saved[layer - 1, b, 1] = w_im
                    nxt.append((w_re * o_re - w_im * o_im, w_re * o_im + w_im * o_re))
                last = layer + 1 == slices
                lhs, rhs = (dft_left, dft_right) if last else (kern_left, kern_right)
                for b, wave in zip(chain, forward_two_sided(lhs[...], rhs[...], nxt)):
                    waves[b] = wave
        grads = list(waves)
        for chain in chains:
            nxt = []
            for b in chain:
                f_re, f_im = waves[b]
                amplitude = jnp.sqrt(f_re * f_re + f_im * f_im + AMP_FLOOR)
                t = target[index[b]].astype(jnp.float32)
                ratio = weight[b] * (amplitude - t) / amplitude
                nxt.append((f_re * ratio, f_im * ratio))
            for b, grad in zip(chain, backward_two_sided(dft_left[...], dft_right[...], nxt)):
                grads[b] = grad
        for layer in reversed(range(slices)):
            for chain in chains:
                nxt = []
                for b in chain:
                    g_re, g_im = grads[b]
                    if layer:
                        w_re, w_im = saved[layer - 1, b, 0], saved[layer - 1, b, 1]
                        o_re, o_im = patches[layer - 1, b, 0], patches[layer - 1, b, 1]
                        nxt.append((o_re * g_re + o_im * g_im, o_re * g_im - o_im * g_re))
                    else:
                        w_re, w_im = probe_ref[0], probe_ref[1]
                    terms = (w_re * g_re + w_im * g_im, w_re * g_im - w_im * g_re)
                    for part in range(2):
                        moved = pltpu.roll(terms[part], forth[b], 1)
                        spot = pl.ds(top[b], patch)
                        acc[part, layer, 0, spot, :] += jnp.where(inside[b], moved, 0.0)
                        acc[part, layer, 1, spot, :] += jnp.where(inside[b], 0.0, moved)
                if layer:
                    for b, grad in zip(chain, backward_two_sided(kern_left[...], kern_right[...], nxt)):
                        grads[b] = grad

    rounds = (mine + BATCH // 2 - 1) // BATCH

    def full(step, carry):
        group(step * BATCH, BATCH)
        return carry

    lax.fori_loop(0, rounds, full, 0)

    @pl.when(rounds * BATCH < mine)
    def _():
        group(rounds * BATCH, BATCH // 2)

    stores = []
    for result, spot in zip((near_keep, near_give, far_keep, far_give), spots):
        for part in range(2):
            for half in range(parts):
                stores.append(
                    pltpu.make_async_copy(
                        acc.at[part, :, half, pl.ds(spot * shard, shard), :],
                        result.at[part, :, :, pl.ds(half * patch, patch)],
                        out_sem.at[len(stores)],
                    )
                )
    for store in stores:
        store.start()
    for store in stores:
        store.wait()


def neighbours():
    tile, pos = lax.axis_index("tile"), lax.axis_index("pos")
    tiles = lax.axis_size("tile")
    sibling = (tile, pos + 1 - 2 * (pos % 2))
    across = (tile, (pos + 2) % 4)
    lower, upper = ((tile + tiles - 1) % tiles, pos), ((tile + 1) % tiles, pos)
    outer = pos < 2
    has_down = jnp.logical_and(outer, tile > 0)
    has_up = jnp.logical_and(outer, tile < tiles - 1)
    return sibling, across, lower, upper, outer, has_down, has_up


def greet(sibling, across, lower, upper, has_down, has_up):
    barrier = pltpu.get_barrier_semaphore()
    mesh_ids = pl.DeviceIdType.MESH
    pl.semaphore_signal(barrier, inc=1, device_id=sibling, device_id_type=mesh_ids)
    pl.semaphore_signal(barrier, inc=1, device_id=across, device_id_type=mesh_ids)

    @pl.when(has_down)
    def _():
        pl.semaphore_signal(barrier, inc=1, device_id=lower, device_id_type=mesh_ids)

    @pl.when(has_up)
    def _():
        pl.semaphore_signal(barrier, inc=1, device_id=upper, device_id_type=mesh_ids)

    pl.semaphore_wait(barrier, 2 + has_down.astype(jnp.int32) + has_up.astype(jnp.int32))


def remote(source, target, send, receive, device):
    return pltpu.make_async_remote_copy(
        src_ref=source, dst_ref=target, send_sem=send, recv_sem=receive,
        device_id=device, device_id_type=pl.DeviceIdType.MESH,
    )


def gather_kernel(
    re_ref, im_ref, near, nearsib, far, farsib,
    near_send, near_recv, far_send, far_recv, pass_send, pass_recv, fpass_send, fpass_recv,
):
    sibling, across, lower, upper, outer, has_down, has_up = neighbours()
    slices = re_ref.shape[0]
    fields = (re_ref, im_ref)
    chunks = list(enumerate((part, layer) for layer in range(slices) for part in range(2)))
    over = [remote(fields[p].at[s], near.at[p, s], near_send.at[k], near_recv.at[k], across) for k, (p, s) in chunks]
    down = [remote(fields[p].at[s], far.at[p, s], far_send.at[k], far_recv.at[k], lower) for k, (p, s) in chunks]
    over_pass = [remote(near.at[p, s], nearsib.at[p, s], pass_send.at[k], pass_recv.at[k], sibling) for k, (p, s) in chunks]
    down_pass = [remote(far.at[p, s], farsib.at[p, s], fpass_send.at[k], fpass_recv.at[k], sibling) for k, (p, s) in chunks]
    own_pass = [remote(fields[p].at[s], farsib.at[p, s], fpass_send.at[k], fpass_recv.at[k], sibling) for k, (p, s) in chunks]
    greet(sibling, across, lower, upper, has_down, has_up)

    @pl.when(has_down)
    def _():
        for one, other in zip(over, down):
            other.start()
            one.start()

    @pl.when(jnp.logical_not(has_down))
    def _():
        for one in over:
            one.start()

    @pl.when(jnp.logical_not(outer))
    def _():
        for copy in own_pass:
            copy.start()

    for k, _ in chunks:
        over[k].wait_recv()
        over_pass[k].start()

        @pl.when(has_up)
        def _():
            down[k].wait_recv()
            down_pass[k].start()

    @pl.when(has_up)
    def _():
        for copy in down_pass:
            copy.wait()

    @pl.when(jnp.logical_not(outer))
    def _():
        for copy in own_pass:
            copy.wait()

    for k, _ in chunks:
        over_pass[k].wait()
        over[k].wait_send()

    @pl.when(has_down)
    def _():
        for copy in down:
            copy.wait_send()


def scatter_kernel(
    near_keep, near_give, far_keep, far_give, from_near, from_far,
    near_kept, near_got, near_sum, far_kept, far_got, far_sum,
    nk_sem, fk_sem, ng_send, ng_recv, fg_send, fg_recv, near_send, near_recv, far_send, far_recv,
):
    sibling, across, lower, upper, outer, has_down, has_up = neighbours()
    slices = near_keep.shape[1]
    chunks = list(enumerate((part, layer) for layer in range(slices) for part in range(2)))
    near_loads = [pltpu.make_async_copy(near_keep.at[p, s], near_kept.at[p, s], nk_sem.at[k]) for k, (p, s) in chunks]
    far_loads = [pltpu.make_async_copy(far_keep.at[p, s], far_kept.at[p, s], fk_sem.at[k]) for k, (p, s) in chunks]
    near_gifts = [remote(near_give.at[p, s], near_got.at[p, s], ng_send.at[k], ng_recv.at[k], sibling) for k, (p, s) in chunks]
    far_gifts = [remote(far_give.at[p, s], far_got.at[p, s], fg_send.at[k], fg_recv.at[k], sibling) for k, (p, s) in chunks]
    over = [remote(near_sum.at[p, s], from_near.at[p, s], near_send.at[k], near_recv.at[k], across) for k, (p, s) in chunks]
    up = [remote(far_sum.at[p, s], from_far.at[p, s], far_send.at[k], far_recv.at[k], upper) for k, (p, s) in chunks]
    hold = [pltpu.make_async_copy(far_sum.at[p, s], from_far.at[p, s], far_send.at[k]) for k, (p, s) in chunks]
    for k, _ in chunks:
        near_loads[k].start()
        far_loads[k].start()
    greet(sibling, across, lower, upper, has_down, has_up)
    for k, _ in chunks:
        near_gifts[k].start()
        far_gifts[k].start()
    for k, (p, s) in chunks:
        near_loads[k].wait()
        near_gifts[k].wait_recv()
        near_sum[p, s] = near_kept[p, s] + near_got[p, s]
        over[k].start()
        far_loads[k].wait()
        far_gifts[k].wait_recv()
        far_sum[p, s] = far_kept[p, s] + far_got[p, s]

        @pl.when(has_up)
        def _():
            up[k].start()

        @pl.when(jnp.logical_not(outer))
        def _():
            hold[k].start()

    for k, _ in chunks:
        near_gifts[k].wait_send()
        far_gifts[k].wait_send()
        over[k].wait()

    @pl.when(jnp.logical_not(outer))
    def _():
        for copy in hold:
            copy.wait()

    @pl.when(has_up)
    def _():
        for copy in up:
            copy.wait_send()

    @pl.when(has_down)
    def _():
        for copy in up:
            copy.wait_recv()


def local(obj_real, obj_imag, probe, fresnel_phase, row_offset, col_offset, live_count, measured):
    slices, shard, width = obj_real.shape
    patch = probe.shape[-1]
    parts = width // patch
    taps = fresnel_phase.shape[0]
    chunks = 2 * slices
    assert lax.axis_size("pos") == 4 and 2 * shard == patch and parts == 2
    block = jax.ShapeDtypeStruct((2, slices, shard, width), jnp.float32)
    smem = pl.BlockSpec(memory_space=pltpu.SMEM)
    vmem = pl.BlockSpec(memory_space=pltpu.VMEM)
    anywhere = pl.BlockSpec(memory_space=pl.ANY)
    dma = pltpu.SemaphoreType.DMA
    near, nearsib, far, farsib = pl.pallas_call(
        gather_kernel,
        out_shape=[block] * 4,
        in_specs=[anywhere] * 2,
        out_specs=[anywhere] * 4,
        scratch_shapes=[dma((chunks,))] * 8,
        compiler_params=pltpu.CompilerParams(
            collective_id=0, has_side_effects=True, vmem_limit_bytes=VMEM_BYTES
        ),
        name="gather_rows",
    )(obj_real, obj_imag)
    phase = jnp.pad(fresnel_phase, (0, patch - taps)).reshape(1, patch)
    dft_left, dft_right = dft_tables(patch)
    parts_of_sum = pl.pallas_call(
        functools.partial(compute_kernel, taps),
        out_shape=[block] * 4,
        in_specs=[smem] * 3 + [vmem] * 4 + [anywhere] * 7,
        out_specs=[anywhere] * 4,
        scratch_shapes=[
            pltpu.VMEM((2, slices, parts, 4 * shard, patch), jnp.float32),
            pltpu.VMEM((2, slices, parts, 4 * shard, patch), jnp.float32),
            pltpu.VMEM(measured.shape, measured.dtype),
            pltpu.VMEM((2 * patch, 2 * patch), jnp.bfloat16),
            pltpu.VMEM((2 * patch, 2 * patch), jnp.bfloat16),
            pltpu.VMEM((slices - 1, BATCH, 2, patch, patch), jnp.float32),
            pltpu.VMEM((slices - 1, BATCH, 2, patch, patch), jnp.float32),
            pltpu.SMEM((row_offset.shape[0] + 8,), jnp.int32),
            pltpu.SemaphoreType.DMA((8 * parts,)),
            pltpu.SemaphoreType.DMA,
            pltpu.SemaphoreType.DMA((8 * parts,)),
        ],
        compiler_params=pltpu.CompilerParams(vmem_limit_bytes=VMEM_BYTES),
        name="patch_gradients",
    )(
        row_offset, col_offset, live_count, phase, dft_left, dft_right, probe,
        obj_real, obj_imag, near, nearsib, far, farsib, measured,
    )
    from_near, from_far = pl.pallas_call(
        scatter_kernel,
        out_shape=[block] * 2,
        in_specs=[anywhere] * 4,
        out_specs=[anywhere] * 2,
        scratch_shapes=[pltpu.VMEM(block.shape, jnp.float32)] * 6 + [dma((chunks,))] * 10,
        compiler_params=pltpu.CompilerParams(
            collective_id=1, has_side_effects=True, vmem_limit_bytes=VMEM_BYTES
        ),
        name="scatter_rows",
    )(*parts_of_sum)
    alone = jnp.logical_and(lax.axis_index("tile") == 0, lax.axis_index("pos") < 2)
    return tuple(from_near[p] + jnp.where(alone, 0.0, from_far[p]) for p in range(2))


def solution(mesh):
    in_specs = (
        P(None, ("tile", "pos"), None),
        P(None, ("tile", "pos"), None),
        P(),
        P(),
        P("tile"),
        P("tile"),
        P("tile"),
        P("tile", None, None),
    )
    out_specs = (P(None, ("tile", "pos"), None), P(None, ("tile", "pos"), None))
    return jax.shard_map(local, mesh=mesh, in_specs=in_specs, out_specs=out_specs, check_vma=False)
```

```python
import functools

import jax
import jax.numpy as jnp
import ml_dtypes
import numpy as np
from jax import lax
from jax.experimental import pallas as pl
from jax.experimental.pallas import tpu as pltpu
from jax.sharding import PartitionSpec as P

AMP_FLOOR = 0.25
BATCH = 4
CHAIN = 2
VMEM_BYTES = 60 * 1024 * 1024


def dft_tables(patch):
    grid = np.arange(patch)
    product = (grid[:, None] * grid[None, :] % patch).astype(np.float32)
    angle = np.float32(2.0 * np.pi / patch) * product
    norm = np.float32(1.0) / np.sqrt(np.float32(patch))
    real = (np.cos(angle) * norm).astype(ml_dtypes.bfloat16)
    imag = (-np.sin(angle) * norm).astype(ml_dtypes.bfloat16)
    left = np.block([[real, -imag], [imag, real]])
    right = np.block([[real.T, imag.T], [-imag.T, real.T]])
    return jnp.asarray(left), jnp.asarray(right)


def dot(left, right):
    return jnp.dot(left, right, preferred_element_type=jnp.float32)


def stack_rows(pairs):
    return jnp.concatenate([jnp.concatenate(pair, axis=0) for pair in pairs], axis=1)


def stack_cols(pairs):
    return jnp.concatenate([jnp.concatenate(pair, axis=1) for pair in pairs], axis=0)


def split_rows(array, patch):
    count = array.shape[1] // patch
    return [
        (array[:patch, b * patch : (b + 1) * patch], array[patch:, b * patch : (b + 1) * patch])
        for b in range(count)
    ]


def split_cols(array, patch):
    count = array.shape[0] // patch
    return [
        (array[b * patch : (b + 1) * patch, :patch], array[b * patch : (b + 1) * patch, patch:])
        for b in range(count)
    ]


def halves(pairs):
    return [(a.astype(jnp.bfloat16), b.astype(jnp.bfloat16)) for a, b in pairs]


def forward_two_sided(left, right, pairs):
    patch = pairs[0][0].shape[0]
    inner = split_rows(dot(left, stack_rows(halves(pairs))), patch)
    return split_cols(dot(stack_cols(halves(inner)), right), patch)


def backward_two_sided(left, right, pairs):
    patch = pairs[0][0].shape[0]
    inner = split_cols(dot(stack_cols(halves(pairs)), left), patch)
    return split_rows(dot(right, stack_rows(halves(inner))), patch)


def compute_kernel(
    taps, rows_ref, cols_ref, live_ref, phase_ref, dft_left, dft_right, probe_ref,
    own_re, own_im, sib_ref, near_ref, nearsib_ref, far_ref, farsib_ref, measured_ref,
    own_keep, own_give, near_keep, near_give, far_keep, far_give,
    window, acc, target, kern_left, kern_right, saved, patches, phases, in_sem, target_sem, out_sem,
):
    slices, shard, width = own_re.shape
    patch = probe_ref.shape[-1]
    slots = rows_ref.shape[0]
    parts = width // patch
    member = lax.axis_index("pos")
    parity = member % 2
    get_target = pltpu.make_async_copy(measured_ref, target, target_sem)
    get_target.start()
    pair = member // 2
    ahead = lax.axis_index("tile") + 1 < lax.axis_size("tile")
    rank = (pair * 2 + parity, pair * 2 + 1 - parity)
    spots = (rank[0], rank[1], 2 - pair * 2 + parity, 3 - pair * 2 - parity, 4 + parity, 5 - parity)

    def loads_of(real, imag, place):
        return [
            pltpu.make_async_copy(
                source.at[:, :, pl.ds(half * patch, patch)],
                window.at[part, :, half, pl.ds(spots[place] * shard, shard), :],
                in_sem.at[(place * 2 + part) * parts + half],
            )
            for part, source in enumerate((real, imag))
            for half in range(parts)
        ]

    near_loads = loads_of(own_re, own_im, 0)
    for place, block in enumerate((sib_ref, near_ref, nearsib_ref)):
        near_loads += loads_of(block.at[0], block.at[1], place + 1)
    far_loads = loads_of(far_ref.at[0], far_ref.at[1], 4)
    far_loads += loads_of(farsib_ref.at[0], farsib_ref.at[1], 5)
    for load in near_loads:
        load.start()

    @pl.when(ahead)
    def _():
        for load in far_loads:
            load.start()

    @pl.when(jnp.logical_not(ahead))
    def _():
        window[:, :, :, 4 * shard :, :] = jnp.zeros(
            window.shape[:3] + (2 * shard, patch), window.dtype
        )

    members = lax.axis_size("pos")
    mine = jnp.maximum(live_ref[0] - member + members - 1, 0) // members

    row = lax.broadcasted_iota(jnp.int32, (patch, patch), 0)
    col = lax.broadcasted_iota(jnp.int32, (patch, patch), 1)
    band = jnp.logical_and(col - row + taps // 2 >= 0, col - row + taps // 2 < taps)
    scale = 1.0 / jnp.sqrt(jnp.float32(taps))

    def toeplitz(values):
        wide = jnp.broadcast_to(values, (patch, patch))
        moved = pltpu.roll(wide, patch - taps // 2, 1, stride=1, stride_axis=0)
        return jnp.where(band, moved, 0.0)

    phases[...] = jnp.zeros_like(phases)
    phases[:, :taps] = phase_ref[...]
    kern_re = toeplitz(jnp.cos(phases[...]) * scale)
    kern_im = toeplitz(jnp.sin(phases[...]) * scale)
    kern_left[...] = stack_rows(halves([(kern_re, kern_im), (-kern_im, kern_re)]))
    kern_re_t, kern_im_t = kern_re.T, kern_im.T
    kern_right[...] = stack_rows(halves([(kern_re_t, -kern_im_t), (kern_im_t, kern_re_t)]))
    acc[...] = jnp.zeros_like(acc)
    for load in near_loads:
        load.wait()

    @pl.when(ahead)
    def _():
        for load in far_loads:
            load.wait()

    get_target.wait()

    def group(first, size):
        every = range(size)
        chains = [list(every)[c : c + CHAIN] for c in range(0, size, CHAIN)]
        index = [member + members * jnp.minimum(first + b, mine - 1) for b in every]
        weight = [(first + b < mine).astype(jnp.float32) for b in every]
        top = [rows_ref[i] for i in index]
        left = [cols_ref[i] for i in index]
        back = [(patch - x) % patch for x in left]
        forth = [x % patch for x in left]
        inside = [col >= x for x in left]

        def cut(layer, b, part):
            a0 = window[part, layer, 0, pl.ds(top[b], patch), :]
            a1 = window[part, layer, 1, pl.ds(top[b], patch), :]
            return pltpu.roll(jnp.where(inside[b], a0, a1), back[b], 1)

        waves = [(probe_ref[0], probe_ref[1]) for _ in every]
        for layer in range(slices):
            for chain in chains:
                nxt = []
                for b in chain:
                    o_re, o_im = cut(layer, b, 0), cut(layer, b, 1)
                    w_re, w_im = waves[b]
                    if layer:
                        patches[layer - 1, b, 0] = o_re
                        patches[layer - 1, b, 1] = o_im
                        saved[layer - 1, b, 0] = w_re
                        saved[layer - 1, b, 1] = w_im
                    nxt.append((w_re * o_re - w_im * o_im, w_re * o_im + w_im * o_re))
                last = layer + 1 == slices
                lhs, rhs = (dft_left, dft_right) if last else (kern_left, kern_right)
                for b, wave in zip(chain, forward_two_sided(lhs[...], rhs[...], nxt)):
                    waves[b] = wave
        grads = list(waves)
        for chain in chains:
            nxt = []
            for b in chain:
                f_re, f_im = waves[b]
                amplitude = jnp.sqrt(f_re * f_re + f_im * f_im + AMP_FLOOR)
                t = target[index[b]].astype(jnp.float32)
                ratio = weight[b] * (amplitude - t) / amplitude
                nxt.append((f_re * ratio, f_im * ratio))
            for b, grad in zip(chain, backward_two_sided(dft_left[...], dft_right[...], nxt)):
                grads[b] = grad
        for layer in reversed(range(slices)):
            for chain in chains:
                nxt = []
                for b in chain:
                    g_re, g_im = grads[b]
                    if layer:
                        w_re, w_im = saved[layer - 1, b, 0], saved[layer - 1, b, 1]
                        o_re, o_im = patches[layer - 1, b, 0], patches[layer - 1, b, 1]
                        nxt.append((o_re * g_re + o_im * g_im, o_re * g_im - o_im * g_re))
                    else:
                        w_re, w_im = probe_ref[0], probe_ref[1]
                    terms = (w_re * g_re + w_im * g_im, w_re * g_im - w_im * g_re)
                    for part in range(2):
                        moved = pltpu.roll(terms[part], forth[b], 1)
                        spot = pl.ds(top[b], patch)
                        acc[part, layer, 0, spot, :] += jnp.where(inside[b], moved, 0.0)
                        acc[part, layer, 1, spot, :] += jnp.where(inside[b], 0.0, moved)
                if layer:
                    for b, grad in zip(chain, backward_two_sided(kern_left[...], kern_right[...], nxt)):
                        grads[b] = grad

    def full(step, carry):
        group(step * BATCH, BATCH)
        return carry

    lax.fori_loop(0, (mine + BATCH - 1) // BATCH, full, 0)

    stores = []
    for result, spot in zip((own_keep, own_give, near_keep, near_give, far_keep, far_give), spots):
        for part in range(2):
            for half in range(parts):
                stores.append(
                    pltpu.make_async_copy(
                        acc.at[part, :, half, pl.ds(spot * shard, shard), :],
                        result.at[part, :, :, pl.ds(half * patch, patch)],
                        out_sem.at[len(stores)],
                    )
                )
    for store in stores:
        store.start()
    for store in stores:
        store.wait()


def neighbours():
    tile, pos = lax.axis_index("tile"), lax.axis_index("pos")
    tiles = lax.axis_size("tile")
    sibling = (tile, pos + 1 - 2 * (pos % 2))
    across = (tile, (pos + 2) % 4)
    lower, upper = ((tile + tiles - 1) % tiles, pos), ((tile + 1) % tiles, pos)
    return sibling, across, lower, upper, pos < 2, tile > 0, tile < tiles - 1


def greet(sibling, across, lower, upper, has_down, has_up):
    barrier = pltpu.get_barrier_semaphore()
    mesh_ids = pl.DeviceIdType.MESH
    pl.semaphore_signal(barrier, inc=1, device_id=sibling, device_id_type=mesh_ids)
    pl.semaphore_signal(barrier, inc=1, device_id=across, device_id_type=mesh_ids)

    @pl.when(has_down)
    def _():
        pl.semaphore_signal(barrier, inc=1, device_id=lower, device_id_type=mesh_ids)

    @pl.when(has_up)
    def _():
        pl.semaphore_signal(barrier, inc=1, device_id=upper, device_id_type=mesh_ids)

    pl.semaphore_wait(barrier, 2 + has_down.astype(jnp.int32) + has_up.astype(jnp.int32))


def remote(source, target, send, receive, device):
    return pltpu.make_async_remote_copy(
        src_ref=source, dst_ref=target, send_sem=send, recv_sem=receive,
        device_id=device, device_id_type=pl.DeviceIdType.MESH,
    )


def gather_kernel(
    re_ref, im_ref, sib, near, nearsib, far, farsib,
    sib_send, sib_recv, near_send, near_recv, far_send, far_recv, pass_send, pass_recv, fpass_send, fpass_recv,
):
    sibling, across, lower, upper, outer, has_down, has_up = neighbours()
    slices = re_ref.shape[0]
    fields = (re_ref, im_ref)
    chunks = list(enumerate((part, layer) for layer in range(slices) for part in range(2)))
    over = [remote(fields[p].at[s], near.at[p, s], near_send.at[k], near_recv.at[k], across) for k, (p, s) in chunks]
    down = [remote(fields[p].at[s], far.at[p, s], far_send.at[k], far_recv.at[k], lower) for k, (p, s) in chunks]
    relay = [remote(near.at[p, s], far.at[p, s], far_send.at[k], far_recv.at[k], lower) for k, (p, s) in chunks]
    over_pass = [remote(near.at[p, s], nearsib.at[p, s], pass_send.at[k], pass_recv.at[k], sibling) for k, (p, s) in chunks]
    down_pass = [remote(far.at[p, s], farsib.at[p, s], fpass_send.at[k], fpass_recv.at[k], sibling) for k, (p, s) in chunks]
    own_pass = [remote(fields[p], sib.at[p], sib_send.at[p], sib_recv.at[p], sibling) for p in range(2)]
    greet(sibling, across, lower, upper, has_down, has_up)
    direct = jnp.logical_and(has_down, outer)
    relayed = jnp.logical_and(has_down, jnp.logical_not(outer))

    for one in over:
        one.start()

    @pl.when(direct)
    def _():
        for other in down:
            other.start()

    for copy in own_pass:
        copy.start()

    for k, _ in chunks:
        over[k].wait_recv()

        @pl.when(relayed)
        def _():
            relay[k].start()

        over_pass[k].start()

    @pl.when(has_up)
    def _():
        for k, _ in chunks:
            down[k].wait_recv()
            down_pass[k].start()
        for copy in down_pass:
            copy.wait()

    for copy in own_pass:
        copy.wait()
    for k, _ in chunks:
        over_pass[k].wait()
        over[k].wait_send()

    @pl.when(has_down)
    def _():
        for copy in down:
            copy.wait_send()


def scatter_kernel(
    own_keep, own_give, near_keep, near_give, far_keep, far_give, from_near, result,
    own_kept, own_got, near_kept, near_got, near_sum, far_kept, far_got, far_sum, behind,
    ok_sem, nk_sem, fk_sem, og_send, og_recv, ng_send, ng_recv, fg_send, fg_recv,
    near_send, near_recv, far_send, far_recv, out_sem,
):
    sibling, across, lower, upper, outer, has_down, has_up = neighbours()
    slices = near_keep.shape[1]
    chunks = list(enumerate((part, layer) for layer in range(slices) for part in range(2)))

    def load(source, target, sem):
        return [pltpu.make_async_copy(source.at[p, s], target.at[p, s], sem.at[k]) for k, (p, s) in chunks]

    def give(source, target, send, recv, device):
        return [remote(source.at[p, s], target.at[p, s], send.at[k], recv.at[k], device) for k, (p, s) in chunks]

    far_loads = load(far_keep, far_kept, fk_sem)
    near_loads = load(near_keep, near_kept, nk_sem)
    own_loads = load(own_keep, own_kept, ok_sem)
    far_gifts = give(far_give, far_got, fg_send, fg_recv, sibling)
    near_gifts = give(near_give, near_got, ng_send, ng_recv, sibling)
    own_gifts = give(own_give, own_got, og_send, og_recv, sibling)
    over = give(near_sum, from_near, near_send, near_recv, across)
    up = give(far_sum, behind, far_send, far_recv, upper)
    stores = load(own_kept, result, out_sem)
    for copies in (far_loads, near_loads, own_loads):
        for copy in copies:
            copy.start()
    greet(sibling, across, lower, upper, has_down, has_up)
    for k, _ in chunks:
        far_gifts[k].start()
        near_gifts[k].start()
    for copy in own_gifts:
        copy.start()

    def send_near(k, extra):
        p, s = chunks[k][1]
        total = near_kept[p, s] + near_got[p, s]
        near_sum[p, s] = total if extra is None else total + extra
        over[k].start()

    for k, (p, s) in chunks:
        far_loads[k].wait()
        far_gifts[k].wait_recv()
        far_sum[p, s] = far_kept[p, s] + far_got[p, s]

        @pl.when(has_up)
        def _():
            up[k].start()

        near_loads[k].wait()
        near_gifts[k].wait_recv()

        @pl.when(outer)
        def _():
            send_near(k, None)

    inner = jnp.logical_not(outer)

    @pl.when(jnp.logical_and(inner, has_down))
    def _():
        for k, (p, s) in chunks:
            up[k].wait_recv()
            send_near(k, behind[p, s])

    @pl.when(jnp.logical_and(inner, jnp.logical_not(has_down)))
    def _():
        for k, _ in chunks:
            send_near(k, None)

    for k, (p, s) in chunks:
        own_loads[k].wait()
        own_gifts[k].wait_recv()
        own_kept[p, s] = own_kept[p, s] + own_got[p, s]

    @pl.when(jnp.logical_and(outer, has_down))
    def _():
        for k, (p, s) in chunks:
            up[k].wait_recv()
            own_kept[p, s] = own_kept[p, s] + behind[p, s]

    for copy in stores:
        copy.start()
    for k, _ in chunks:
        far_gifts[k].wait_send()
        near_gifts[k].wait_send()
        own_gifts[k].wait_send()
        over[k].wait()

    @pl.when(has_up)
    def _():
        for copy in up:
            copy.wait_send()

    for copy in stores:
        copy.wait()


def local(obj_real, obj_imag, probe, fresnel_phase, row_offset, col_offset, live_count, measured):
    slices, shard, width = obj_real.shape
    patch = probe.shape[-1]
    parts = width // patch
    taps = fresnel_phase.shape[0]
    chunks = 2 * slices
    assert lax.axis_size("pos") == 4 and 2 * shard == patch and parts == 2
    block = jax.ShapeDtypeStruct((2, slices, shard, width), jnp.float32)
    smem = pl.BlockSpec(memory_space=pltpu.SMEM)
    vmem = pl.BlockSpec(memory_space=pltpu.VMEM)
    anywhere = pl.BlockSpec(memory_space=pl.ANY)
    dma = pltpu.SemaphoreType.DMA
    fetched = pl.pallas_call(
        gather_kernel,
        out_shape=[block] * 5,
        in_specs=[anywhere] * 2,
        out_specs=[anywhere] * 5,
        scratch_shapes=[dma((2,))] * 2 + [dma((chunks,))] * 8,
        compiler_params=pltpu.CompilerParams(
            collective_id=0, has_side_effects=True, vmem_limit_bytes=VMEM_BYTES
        ),
        name="gather_rows",
    )(obj_real, obj_imag)
    phase = fresnel_phase.reshape(1, taps)
    dft_left, dft_right = dft_tables(patch)
    parts_of_sum = pl.pallas_call(
        functools.partial(compute_kernel, taps),
        out_shape=[block] * 6,
        in_specs=[smem] * 3 + [vmem] * 4 + [anywhere] * 8,
        out_specs=[anywhere] * 6,
        scratch_shapes=[
            pltpu.VMEM((2, slices, parts, 6 * shard, patch), jnp.float32),
            pltpu.VMEM((2, slices, parts, 6 * shard, patch), jnp.float32),
            pltpu.VMEM(measured.shape, measured.dtype),
            pltpu.VMEM((2 * patch, 2 * patch), jnp.bfloat16),
            pltpu.VMEM((2 * patch, 2 * patch), jnp.bfloat16),
            pltpu.VMEM((slices - 1, BATCH, 2, patch, patch), jnp.float32),
            pltpu.VMEM((slices - 1, BATCH, 2, patch, patch), jnp.float32),
            pltpu.VMEM((1, patch), jnp.float32),
            pltpu.SemaphoreType.DMA((12 * parts,)),
            pltpu.SemaphoreType.DMA,
            pltpu.SemaphoreType.DMA((12 * parts,)),
        ],
        compiler_params=pltpu.CompilerParams(vmem_limit_bytes=VMEM_BYTES),
        name="patch_gradients",
    )(
        row_offset, col_offset, live_count, phase, dft_left, dft_right, probe,
        obj_real, obj_imag, *fetched, measured,
    )
    from_near, rest = pl.pallas_call(
        scatter_kernel,
        out_shape=[block] * 2,
        in_specs=[anywhere] * 6,
        out_specs=[anywhere] * 2,
        scratch_shapes=[pltpu.VMEM(block.shape, jnp.float32)] * 9 + [dma((chunks,))] * 14,
        compiler_params=pltpu.CompilerParams(
            collective_id=1, has_side_effects=True, vmem_limit_bytes=VMEM_BYTES
        ),
        name="scatter_rows",
    )(*parts_of_sum)
    return tuple(from_near[p] + rest[p] for p in range(2))


def solution(mesh):
    in_specs = (
        P(None, ("tile", "pos"), None),
        P(None, ("tile", "pos"), None),
        P(),
        P(),
        P("tile"),
        P("tile"),
        P("tile"),
        P("tile", None, None),
    )
    out_specs = (P(None, ("tile", "pos"), None), P(None, ("tile", "pos"), None))
    return jax.shard_map(local, mesh=mesh, in_specs=in_specs, out_specs=out_specs, check_vma=False)
```

```python
import functools

import jax
import jax.numpy as jnp
import ml_dtypes
import numpy as np
from jax import lax
from jax.experimental import pallas as pl
from jax.experimental.pallas import tpu as pltpu
from jax.sharding import PartitionSpec as P

AMP_FLOOR = 0.25
BATCH = 8
CHAIN = 2
VMEM_BYTES = 60 * 1024 * 1024


def dft_tables(patch):
    grid = np.arange(patch)
    product = (grid[:, None] * grid[None, :] % patch).astype(np.float32)
    angle = np.float32(2.0 * np.pi / patch) * product
    norm = np.float32(1.0) / np.sqrt(np.float32(patch))
    real = (np.cos(angle) * norm).astype(ml_dtypes.bfloat16)
    imag = (-np.sin(angle) * norm).astype(ml_dtypes.bfloat16)
    left = np.block([[real, -imag], [imag, real]])
    right = np.block([[real.T, imag.T], [-imag.T, real.T]])
    return jnp.asarray(left), jnp.asarray(right)


def dot(left, right):
    return jnp.dot(left, right, preferred_element_type=jnp.float32)


def stack_rows(pairs):
    return jnp.concatenate([jnp.concatenate(pair, axis=0) for pair in pairs], axis=1)


def stack_cols(pairs):
    return jnp.concatenate([jnp.concatenate(pair, axis=1) for pair in pairs], axis=0)


def split_rows(array, patch):
    count = array.shape[1] // patch
    return [
        (array[:patch, b * patch : (b + 1) * patch], array[patch:, b * patch : (b + 1) * patch])
        for b in range(count)
    ]


def split_cols(array, patch):
    count = array.shape[0] // patch
    return [
        (array[b * patch : (b + 1) * patch, :patch], array[b * patch : (b + 1) * patch, patch:])
        for b in range(count)
    ]


def halves(pairs):
    return [(a.astype(jnp.bfloat16), b.astype(jnp.bfloat16)) for a, b in pairs]


def forward_two_sided(left, right, pairs):
    patch = pairs[0][0].shape[0]
    inner = split_rows(dot(left, stack_rows(halves(pairs))), patch)
    return split_cols(dot(stack_cols(halves(inner)), right), patch)


def backward_two_sided(left, right, pairs):
    patch = pairs[0][0].shape[0]
    inner = split_cols(dot(stack_cols(halves(pairs)), left), patch)
    return split_rows(dot(right, stack_rows(halves(inner))), patch)


def compute_kernel(
    taps, rows_ref, cols_ref, live_ref, phase_ref, dft_left, dft_right, probe_ref,
    own_re, own_im, near_ref, nearsib_ref, far_ref, farsib_ref, measured_ref,
    near_keep, near_give, far_keep, far_give,
    window, acc, target, kern_left, kern_right, saved, patches, phases, listed, in_sem, target_sem, out_sem,
):
    slices, shard, width = own_re.shape
    patch = probe_ref.shape[-1]
    slots = rows_ref.shape[0]
    parts = width // patch
    member = lax.axis_index("pos")
    parity = member % 2

    def get_target(item, slot):
        return pltpu.make_async_copy(measured_ref.at[slot], target.at[item], target_sem.at[item])

    outer = member < 2
    ahead = jnp.logical_and(outer, lax.axis_index("tile") + 1 < lax.axis_size("tile"))
    base = jnp.where(outer, 2 * shard, 0)
    spots = (parity, 1 - parity, 2 + parity, 3 - parity)

    def loads_of(real, imag, place):
        return [
            pltpu.make_async_copy(
                source.at[:, :, pl.ds(half * patch, patch)],
                window.at[part, :, half, pl.ds(spots[place] * shard, shard), :],
                in_sem.at[(place * 2 + part) * parts + half],
            )
            for part, source in enumerate((real, imag))
            for half in range(parts)
        ]

    near_loads = loads_of(near_ref.at[0], near_ref.at[1], 0)
    near_loads += loads_of(nearsib_ref.at[0], nearsib_ref.at[1], 1)
    own_loads = loads_of(own_re, own_im, 2)
    far_loads = loads_of(far_ref.at[0], far_ref.at[1], 2)
    farsib_loads = loads_of(farsib_ref.at[0], farsib_ref.at[1], 3)
    for load in near_loads:
        load.start()

    @pl.when(jnp.logical_not(outer))
    def _():
        for load in own_loads + farsib_loads:
            load.start()

    @pl.when(ahead)
    def _():
        for load in far_loads + farsib_loads:
            load.start()

    @pl.when(jnp.logical_and(outer, jnp.logical_not(ahead)))
    def _():
        window[:, :, :, 2 * shard :, :] = jnp.zeros(
            window.shape[:3] + (2 * shard, patch), window.dtype
        )

    def pick(slot, count):
        ok = jnp.logical_and(slot < live_ref[0], (rows_ref[slot] >= 2 * shard) == outer)
        take = jnp.logical_and(ok, count % 2 == parity)
        listed[jnp.where(take, count // 2, slots)] = slot
        return count + ok.astype(jnp.int32)

    total = lax.fori_loop(0, slots, pick, jnp.int32(0))
    mine = (total + 1 - parity) // 2

    def fetch(item, carry):
        get_target(item, listed[item]).start()
        return carry

    lax.fori_loop(0, mine, fetch, 0)

    row = lax.broadcasted_iota(jnp.int32, (patch, patch), 0)
    col = lax.broadcasted_iota(jnp.int32, (patch, patch), 1)
    band = jnp.logical_and(col - row + taps // 2 >= 0, col - row + taps // 2 < taps)
    scale = 1.0 / jnp.sqrt(jnp.float32(taps))

    def toeplitz(values):
        wide = jnp.broadcast_to(values, (patch, patch))
        moved = pltpu.roll(wide, patch - taps // 2, 1, stride=1, stride_axis=0)
        return jnp.where(band, moved, 0.0)

    phases[...] = jnp.zeros_like(phases)
    phases[:, :taps] = phase_ref[...]
    kern_re = toeplitz(jnp.cos(phases[...]) * scale)
    kern_im = toeplitz(jnp.sin(phases[...]) * scale)
    kern_left[...] = stack_rows(halves([(kern_re, kern_im), (-kern_im, kern_re)]))
    kern_re_t, kern_im_t = kern_re.T, kern_im.T
    kern_right[...] = stack_rows(halves([(kern_re_t, -kern_im_t), (kern_im_t, kern_re_t)]))
    acc[...] = jnp.zeros_like(acc)
    for load in near_loads:
        load.wait()

    @pl.when(jnp.logical_or(jnp.logical_not(outer), ahead))
    def _():
        for load in far_loads + farsib_loads:
            load.wait()

    def group(first, size):
        def arrive(item, carry):
            get_target(item, listed[item]).wait()
            return carry

        lax.fori_loop(first, jnp.minimum(first + size, mine), arrive, 0)
        every = range(size)
        chains = [list(every)[c : c + CHAIN] for c in range(0, size, CHAIN)]
        item = [jnp.minimum(first + b, mine - 1) for b in every]
        index = [listed[i] for i in item]
        weight = [(first + b < mine).astype(jnp.float32) for b in every]
        top = [rows_ref[i] - base for i in index]
        left = [cols_ref[i] for i in index]
        back = [(patch - x) % patch for x in left]
        forth = [x % patch for x in left]
        inside = [col >= x for x in left]

        def cut(layer, b, part):
            a0 = window[part, layer, 0, pl.ds(top[b], patch), :]
            a1 = window[part, layer, 1, pl.ds(top[b], patch), :]
            return pltpu.roll(jnp.where(inside[b], a0, a1), back[b], 1)

        waves = [(probe_ref[0], probe_ref[1]) for _ in every]
        for layer in range(slices):
            for chain in chains:
                nxt = []
                for b in chain:
                    o_re, o_im = cut(layer, b, 0), cut(layer, b, 1)
                    w_re, w_im = waves[b]
                    if layer:
                        patches[layer - 1, b, 0] = o_re
                        patches[layer - 1, b, 1] = o_im
                        saved[layer - 1, b, 0] = w_re
                        saved[layer - 1, b, 1] = w_im
                    nxt.append((w_re * o_re - w_im * o_im, w_re * o_im + w_im * o_re))
                last = layer + 1 == slices
                lhs, rhs = (dft_left, dft_right) if last else (kern_left, kern_right)
                for b, wave in zip(chain, forward_two_sided(lhs[...], rhs[...], nxt)):
                    waves[b] = wave
        grads = list(waves)
        for chain in chains:
            nxt = []
            for b in chain:
                f_re, f_im = waves[b]
                amplitude = jnp.sqrt(f_re * f_re + f_im * f_im + AMP_FLOOR)
                t = target[item[b]].astype(jnp.float32)
                ratio = weight[b] * (amplitude - t) / amplitude
                nxt.append((f_re * ratio, f_im * ratio))
            for b, grad in zip(chain, backward_two_sided(dft_left[...], dft_right[...], nxt)):
                grads[b] = grad
        for layer in reversed(range(slices)):
            for chain in chains:
                nxt = []
                for b in chain:
                    g_re, g_im = grads[b]
                    if layer:
                        w_re, w_im = saved[layer - 1, b, 0], saved[layer - 1, b, 1]
                        o_re, o_im = patches[layer - 1, b, 0], patches[layer - 1, b, 1]
                        nxt.append((o_re * g_re + o_im * g_im, o_re * g_im - o_im * g_re))
                    else:
                        w_re, w_im = probe_ref[0], probe_ref[1]
                    terms = (w_re * g_re + w_im * g_im, w_re * g_im - w_im * g_re)
                    for part in range(2):
                        moved = pltpu.roll(terms[part], forth[b], 1)
                        spot = pl.ds(top[b], patch)
                        acc[part, layer, 0, spot, :] += jnp.where(inside[b], moved, 0.0)
                        acc[part, layer, 1, spot, :] += jnp.where(inside[b], 0.0, moved)
                if layer:
                    for b, grad in zip(chain, backward_two_sided(kern_left[...], kern_right[...], nxt)):
                        grads[b] = grad

    rounds = (mine + 1) // BATCH
    rest = mine - rounds * BATCH
    most = jnp.where(rest > BATCH // 4, BATCH // 2, 0)

    def full(step, carry):
        group(step * BATCH, BATCH)
        return carry

    lax.fori_loop(0, rounds, full, 0)

    @pl.when(most > 0)
    def _():
        group(rounds * BATCH, BATCH // 2)

    @pl.when(rest > most)
    def _():
        group(rounds * BATCH + most, BATCH // 4)

    stores = []
    for result, spot in zip((near_keep, near_give, far_keep, far_give), spots):
        for part in range(2):
            for half in range(parts):
                stores.append(
                    pltpu.make_async_copy(
                        acc.at[part, :, half, pl.ds(spot * shard, shard), :],
                        result.at[part, :, :, pl.ds(half * patch, patch)],
                        out_sem.at[len(stores)],
                    )
                )
    for store in stores:
        store.start()
    for store in stores:
        store.wait()


def neighbours():
    tile, pos = lax.axis_index("tile"), lax.axis_index("pos")
    tiles = lax.axis_size("tile")
    sibling = (tile, pos + 1 - 2 * (pos % 2))
    across = (tile, (pos + 2) % 4)
    lower, upper = ((tile + tiles - 1) % tiles, pos), ((tile + 1) % tiles, pos)
    outer = pos < 2
    has_down = jnp.logical_and(outer, tile > 0)
    has_up = jnp.logical_and(outer, tile < tiles - 1)
    return sibling, across, lower, upper, outer, has_down, has_up


def greet(sibling, across, lower, upper, has_down, has_up):
    barrier = pltpu.get_barrier_semaphore()
    mesh_ids = pl.DeviceIdType.MESH
    pl.semaphore_signal(barrier, inc=1, device_id=sibling, device_id_type=mesh_ids)
    pl.semaphore_signal(barrier, inc=1, device_id=across, device_id_type=mesh_ids)

    @pl.when(has_down)
    def _():
        pl.semaphore_signal(barrier, inc=1, device_id=lower, device_id_type=mesh_ids)

    @pl.when(has_up)
    def _():
        pl.semaphore_signal(barrier, inc=1, device_id=upper, device_id_type=mesh_ids)

    pl.semaphore_wait(barrier, 2 + has_down.astype(jnp.int32) + has_up.astype(jnp.int32))


def remote(source, target, send, receive, device):
    return pltpu.make_async_remote_copy(
        src_ref=source, dst_ref=target, send_sem=send, recv_sem=receive,
        device_id=device, device_id_type=pl.DeviceIdType.MESH,
    )


def gather_kernel(
    re_ref, im_ref, near, nearsib, far, farsib,
    near_send, near_recv, far_send, far_recv, pass_send, pass_recv, fpass_send, fpass_recv,
):
    sibling, across, lower, upper, outer, has_down, has_up = neighbours()
    slices = re_ref.shape[0]
    fields = (re_ref, im_ref)
    chunks = list(enumerate((part, layer) for layer in range(slices) for part in range(2)))
    over = [remote(fields[p].at[s], near.at[p, s], near_send.at[k], near_recv.at[k], across) for k, (p, s) in chunks]
    down = [remote(fields[p].at[s], far.at[p, s], far_send.at[k], far_recv.at[k], lower) for k, (p, s) in chunks]
    over_pass = [remote(near.at[p, s], nearsib.at[p, s], pass_send.at[k], pass_recv.at[k], sibling) for k, (p, s) in chunks]
    down_pass = [remote(far.at[p, s], farsib.at[p, s], fpass_send.at[k], fpass_recv.at[k], sibling) for k, (p, s) in chunks]
    own_pass = [remote(fields[p].at[s], farsib.at[p, s], fpass_send.at[k], fpass_recv.at[k], sibling) for k, (p, s) in chunks]
    greet(sibling, across, lower, upper, has_down, has_up)

    @pl.when(has_down)
    def _():
        for one, other in zip(over, down):
            other.start()
            one.start()

    @pl.when(jnp.logical_not(has_down))
    def _():
        for one in over:
            one.start()

    @pl.when(jnp.logical_not(outer))
    def _():
        for copy in own_pass:
            copy.start()

    for k, _ in chunks:
        over[k].wait_recv()
        over_pass[k].start()

        @pl.when(has_up)
        def _():
            down[k].wait_recv()
            down_pass[k].start()

    @pl.when(has_up)
    def _():
        for copy in down_pass:
            copy.wait()

    @pl.when(jnp.logical_not(outer))
    def _():
        for copy in own_pass:
            copy.wait()

    for k, _ in chunks:
        over_pass[k].wait()
        over[k].wait_send()

    @pl.when(has_down)
    def _():
        for copy in down:
            copy.wait_send()


def scatter_kernel(
    near_keep, near_give, far_keep, far_give, from_near, from_far,
    near_kept, near_got, near_sum, far_kept, far_got, far_sum,
    nk_sem, fk_sem, ng_send, ng_recv, fg_send, fg_recv, near_send, near_recv, far_send, far_recv,
):
    sibling, across, lower, upper, outer, has_down, has_up = neighbours()
    slices = near_keep.shape[1]
    chunks = list(enumerate((part, layer) for layer in range(slices) for part in range(2)))
    near_loads = [pltpu.make_async_copy(near_keep.at[p, s], near_kept.at[p, s], nk_sem.at[k]) for k, (p, s) in chunks]
    far_loads = [pltpu.make_async_copy(far_keep.at[p, s], far_kept.at[p, s], fk_sem.at[k]) for k, (p, s) in chunks]
    near_gifts = [remote(near_give.at[p, s], near_got.at[p, s], ng_send.at[k], ng_recv.at[k], sibling) for k, (p, s) in chunks]
    far_gifts = [remote(far_give.at[p, s], far_got.at[p, s], fg_send.at[k], fg_recv.at[k], sibling) for k, (p, s) in chunks]
    over = [remote(near_sum.at[p, s], from_near.at[p, s], near_send.at[k], near_recv.at[k], across) for k, (p, s) in chunks]
    up = [remote(far_sum.at[p, s], from_far.at[p, s], far_send.at[k], far_recv.at[k], upper) for k, (p, s) in chunks]
    hold = [pltpu.make_async_copy(far_sum.at[p, s], from_far.at[p, s], far_send.at[k]) for k, (p, s) in chunks]
    for k, _ in chunks:
        near_loads[k].start()
        far_loads[k].start()
    greet(sibling, across, lower, upper, has_down, has_up)
    for k, _ in chunks:
        near_gifts[k].start()
        far_gifts[k].start()
    for k, (p, s) in chunks:
        near_loads[k].wait()
        near_gifts[k].wait_recv()
        near_sum[p, s] = near_kept[p, s] + near_got[p, s]
        over[k].start()
        far_loads[k].wait()
        far_gifts[k].wait_recv()
        far_sum[p, s] = far_kept[p, s] + far_got[p, s]

        @pl.when(has_up)
        def _():
            up[k].start()

        @pl.when(jnp.logical_not(outer))
        def _():
            hold[k].start()

    for k, _ in chunks:
        near_gifts[k].wait_send()
        far_gifts[k].wait_send()
        over[k].wait()

    @pl.when(jnp.logical_not(outer))
    def _():
        for copy in hold:
            copy.wait()

    @pl.when(has_up)
    def _():
        for copy in up:
            copy.wait_send()

    @pl.when(has_down)
    def _():
        for copy in up:
            copy.wait_recv()


def join_kernel(near, far, out_re, out_im):
    alone = jnp.logical_and(lax.axis_index("tile") == 0, lax.axis_index("pos") < 2)
    out_re[...] = near[0] + jnp.where(alone, 0.0, far[0])
    out_im[...] = near[1] + jnp.where(alone, 0.0, far[1])


def local(obj_real, obj_imag, probe, fresnel_phase, row_offset, col_offset, live_count, measured):
    slices, shard, width = obj_real.shape
    patch = probe.shape[-1]
    parts = width // patch
    taps = fresnel_phase.shape[0]
    chunks = 2 * slices
    assert lax.axis_size("pos") == 4 and 2 * shard == patch and parts == 2
    block = jax.ShapeDtypeStruct((2, slices, shard, width), jnp.float32)
    smem = pl.BlockSpec(memory_space=pltpu.SMEM)
    vmem = pl.BlockSpec(memory_space=pltpu.VMEM)
    anywhere = pl.BlockSpec(memory_space=pl.ANY)
    dma = pltpu.SemaphoreType.DMA
    near, nearsib, far, farsib = pl.pallas_call(
        gather_kernel,
        out_shape=[block] * 4,
        in_specs=[anywhere] * 2,
        out_specs=[anywhere] * 4,
        scratch_shapes=[dma((chunks,))] * 8,
        compiler_params=pltpu.CompilerParams(
            collective_id=0, has_side_effects=True, vmem_limit_bytes=VMEM_BYTES
        ),
        name="gather_rows",
    )(obj_real, obj_imag)
    phase = fresnel_phase.reshape(1, taps)
    dft_left, dft_right = dft_tables(patch)
    parts_of_sum = pl.pallas_call(
        functools.partial(compute_kernel, taps),
        out_shape=[block] * 4,
        in_specs=[smem] * 3 + [vmem] * 4 + [anywhere] * 7,
        out_specs=[anywhere] * 4,
        scratch_shapes=[
            pltpu.VMEM((2, slices, parts, 4 * shard, patch), jnp.float32),
            pltpu.VMEM((2, slices, parts, 4 * shard, patch), jnp.float32),
            pltpu.VMEM((measured.shape[0] // 2,) + measured.shape[1:], measured.dtype),
            pltpu.VMEM((2 * patch, 2 * patch), jnp.bfloat16),
            pltpu.VMEM((2 * patch, 2 * patch), jnp.bfloat16),
            pltpu.VMEM((slices - 1, BATCH, 2, patch, patch), jnp.float32),
            pltpu.VMEM((slices - 1, BATCH, 2, patch, patch), jnp.float32),
            pltpu.VMEM((1, patch), jnp.float32),
            pltpu.SMEM((row_offset.shape[0] + 8,), jnp.int32),
            pltpu.SemaphoreType.DMA((8 * parts,)),
            pltpu.SemaphoreType.DMA((measured.shape[0] // 2,)),
            pltpu.SemaphoreType.DMA((8 * parts,)),
        ],
        compiler_params=pltpu.CompilerParams(vmem_limit_bytes=VMEM_BYTES),
        name="patch_gradients",
    )(
        row_offset, col_offset, live_count, phase, dft_left, dft_right, probe,
        obj_real, obj_imag, near, nearsib, far, farsib, measured,
    )
    from_near, from_far = pl.pallas_call(
        scatter_kernel,
        out_shape=[block] * 2,
        in_specs=[anywhere] * 4,
        out_specs=[anywhere] * 2,
        scratch_shapes=[pltpu.VMEM(block.shape, jnp.float32)] * 6 + [dma((chunks,))] * 10,
        compiler_params=pltpu.CompilerParams(
            collective_id=1, has_side_effects=True, vmem_limit_bytes=VMEM_BYTES
        ),
        name="scatter_rows",
    )(*parts_of_sum)
    pair_block = pl.BlockSpec((2, 1, shard, width), lambda layer: (0, layer, 0, 0))
    one_block = pl.BlockSpec((1, shard, width), lambda layer: (layer, 0, 0))
    return tuple(
        pl.pallas_call(
            join_kernel,
            out_shape=[jax.ShapeDtypeStruct(obj_real.shape, jnp.float32)] * 2,
            grid=(slices,),
            in_specs=[pair_block] * 2,
            out_specs=[one_block] * 2,
            compiler_params=pltpu.CompilerParams(vmem_limit_bytes=VMEM_BYTES),
            name="join_rows",
        )(from_near, from_far)
    )


def solution(mesh):
    in_specs = (
        P(None, ("tile", "pos"), None),
        P(None, ("tile", "pos"), None),
        P(),
        P(),
        P("tile"),
        P("tile"),
        P("tile"),
        P("tile", None, None),
    )
    out_specs = (P(None, ("tile", "pos"), None), P(None, ("tile", "pos"), None))
    return jax.shard_map(local, mesh=mesh, in_specs=in_specs, out_specs=out_specs, check_vma=False)
```

```python
import functools

import jax
import jax.numpy as jnp
import ml_dtypes
import numpy as np
from jax import lax
from jax.experimental import pallas as pl
from jax.experimental.pallas import tpu as pltpu
from jax.sharding import PartitionSpec as P

AMP_FLOOR = 0.25
BATCH = 8
CHAIN = 2
VMEM_BYTES = 60 * 1024 * 1024


def dft_tables(patch):
    grid = np.arange(patch)
    product = (grid[:, None] * grid[None, :] % patch).astype(np.float32)
    angle = np.float32(2.0 * np.pi / patch) * product
    norm = np.float32(1.0) / np.sqrt(np.float32(patch))
    real = (np.cos(angle) * norm).astype(ml_dtypes.bfloat16)
    imag = (-np.sin(angle) * norm).astype(ml_dtypes.bfloat16)
    left = np.block([[real, -imag], [imag, real]])
    right = np.block([[real.T, imag.T], [-imag.T, real.T]])
    return jnp.asarray(left), jnp.asarray(right)


def dot(left, right):
    return jnp.dot(left, right, preferred_element_type=jnp.float32)


def stack_rows(pairs):
    return jnp.concatenate([jnp.concatenate(pair, axis=0) for pair in pairs], axis=1)


def stack_cols(pairs):
    return jnp.concatenate([jnp.concatenate(pair, axis=1) for pair in pairs], axis=0)


def split_rows(array, patch):
    count = array.shape[1] // patch
    return [
        (array[:patch, b * patch : (b + 1) * patch], array[patch:, b * patch : (b + 1) * patch])
        for b in range(count)
    ]


def split_cols(array, patch):
    count = array.shape[0] // patch
    return [
        (array[b * patch : (b + 1) * patch, :patch], array[b * patch : (b + 1) * patch, patch:])
        for b in range(count)
    ]


def halves(pairs):
    return [(a.astype(jnp.bfloat16), b.astype(jnp.bfloat16)) for a, b in pairs]


def forward_two_sided(left, right, pairs):
    patch = pairs[0][0].shape[0]
    inner = split_rows(dot(left, stack_rows(halves(pairs))), patch)
    return split_cols(dot(stack_cols(halves(inner)), right), patch)


def backward_two_sided(left, right, pairs):
    patch = pairs[0][0].shape[0]
    inner = split_cols(dot(stack_cols(halves(pairs)), left), patch)
    return split_rows(dot(right, stack_rows(halves(inner))), patch)


def compute_kernel(
    taps, rows_ref, cols_ref, live_ref, phase_ref, dft_left, dft_right, probe_ref,
    own_re, own_im, near_ref, nearsib_ref, far_ref, farsib_ref, measured_ref,
    near_keep, near_give, far_keep, far_give,
    window, acc, target, kern_left, kern_right, saved, phases, listed, in_sem, target_sem, out_sem,
):
    slices, shard, width = own_re.shape
    patch = probe_ref.shape[-1]
    slots = rows_ref.shape[0]
    parts = width // patch
    member = lax.axis_index("pos")
    parity = member % 2

    def get_target(item, slot):
        return pltpu.make_async_copy(measured_ref.at[slot], target.at[item], target_sem.at[item])

    outer = member < 2
    ahead = jnp.logical_and(outer, lax.axis_index("tile") + 1 < lax.axis_size("tile"))
    base = jnp.where(outer, 2 * shard, 0)
    spots = (parity, 1 - parity, 2 + parity, 3 - parity)

    def loads_of(real, imag, place):
        return [
            pltpu.make_async_copy(
                source.at[:, :, pl.ds(half * patch, patch)],
                window.at[part, :, half, pl.ds(spots[place] * shard, shard), :],
                in_sem.at[(place * 2 + part) * parts + half],
            )
            for part, source in enumerate((real, imag))
            for half in range(parts)
        ]

    near_loads = loads_of(near_ref.at[0], near_ref.at[1], 0)
    near_loads += loads_of(nearsib_ref.at[0], nearsib_ref.at[1], 1)
    own_loads = loads_of(own_re, own_im, 2)
    far_loads = loads_of(far_ref.at[0], far_ref.at[1], 2)
    farsib_loads = loads_of(farsib_ref.at[0], farsib_ref.at[1], 3)
    for load in near_loads:
        load.start()

    @pl.when(jnp.logical_not(outer))
    def _():
        for load in own_loads + farsib_loads:
            load.start()

    @pl.when(ahead)
    def _():
        for load in far_loads + farsib_loads:
            load.start()

    @pl.when(jnp.logical_and(outer, jnp.logical_not(ahead)))
    def _():
        window[:, :, :, 2 * shard :, :] = jnp.zeros(
            window.shape[:3] + (2 * shard, patch), window.dtype
        )

    def pick(slot, count):
        ok = jnp.logical_and(slot < live_ref[0], (rows_ref[slot] >= 2 * shard) == outer)
        take = jnp.logical_and(ok, count % 2 == parity)
        listed[jnp.where(take, count // 2, slots)] = slot
        return count + ok.astype(jnp.int32)

    total = lax.fori_loop(0, slots, pick, jnp.int32(0))
    mine = (total + 1 - parity) // 2

    def fetch(item, carry):
        get_target(item, listed[item]).start()
        return carry

    lax.fori_loop(0, mine, fetch, 0)

    row = lax.broadcasted_iota(jnp.int32, (patch, patch), 0)
    col = lax.broadcasted_iota(jnp.int32, (patch, patch), 1)
    band = jnp.logical_and(col - row + taps // 2 >= 0, col - row + taps // 2 < taps)
    scale = 1.0 / jnp.sqrt(jnp.float32(taps))

    def toeplitz(values):
        wide = jnp.broadcast_to(values, (patch, patch))
        moved = pltpu.roll(wide, patch - taps // 2, 1, stride=1, stride_axis=0)
        return jnp.where(band, moved, 0.0)

    phases[...] = jnp.zeros_like(phases)
    phases[:, :taps] = phase_ref[...]
    kern_re = toeplitz(jnp.cos(phases[...]) * scale)
    kern_im = toeplitz(jnp.sin(phases[...]) * scale)
    kern_left[...] = stack_rows(halves([(kern_re, kern_im), (-kern_im, kern_re)]))
    kern_re_t, kern_im_t = kern_re.T, kern_im.T
    kern_right[...] = stack_rows(halves([(kern_re_t, -kern_im_t), (kern_im_t, kern_re_t)]))
    acc[...] = jnp.zeros_like(acc)
    for load in near_loads:
        load.wait()

    @pl.when(jnp.logical_or(jnp.logical_not(outer), ahead))
    def _():
        for load in far_loads + farsib_loads:
            load.wait()

    def group(first, size):
        def arrive(item, carry):
            get_target(item, listed[item]).wait()
            return carry

        lax.fori_loop(first, jnp.minimum(first + size, mine), arrive, 0)
        every = range(size)
        chains = [list(every)[c : c + CHAIN] for c in range(0, size, CHAIN)]
        item = [jnp.minimum(first + b, mine - 1) for b in every]
        index = [listed[i] for i in item]
        weight = [(first + b < mine).astype(jnp.float32) for b in every]
        top = [rows_ref[i] - base for i in index]
        left = [cols_ref[i] for i in index]
        back = [(patch - x) % patch for x in left]
        forth = [x % patch for x in left]
        inside = [col >= x for x in left]

        def cut(layer, b, part):
            a0 = window[part, layer, 0, pl.ds(top[b], patch), :]
            a1 = window[part, layer, 1, pl.ds(top[b], patch), :]
            return pltpu.roll(jnp.where(inside[b], a0, a1), back[b], 1)

        waves = [(probe_ref[0], probe_ref[1]) for _ in every]
        for layer in range(slices):
            for chain in chains:
                nxt = []
                for b in chain:
                    o_re, o_im = cut(layer, b, 0), cut(layer, b, 1)
                    w_re, w_im = waves[b]
                    if layer:
                        saved[layer - 1, b, 0] = w_re
                        saved[layer - 1, b, 1] = w_im
                    nxt.append((w_re * o_re - w_im * o_im, w_re * o_im + w_im * o_re))
                last = layer + 1 == slices
                lhs, rhs = (dft_left, dft_right) if last else (kern_left, kern_right)
                for b, wave in zip(chain, forward_two_sided(lhs[...], rhs[...], nxt)):
                    waves[b] = wave
        grads = list(waves)
        for chain in chains:
            nxt = []
            for b in chain:
                f_re, f_im = waves[b]
                inverse = lax.rsqrt(f_re * f_re + f_im * f_im + AMP_FLOOR)
                t = target[item[b]].astype(jnp.float32)
                ratio = weight[b] * (1.0 - t * inverse)
                nxt.append((f_re * ratio, f_im * ratio))
            for b, grad in zip(chain, backward_two_sided(dft_left[...], dft_right[...], nxt)):
                grads[b] = grad
        for layer in reversed(range(slices)):
            for chain in chains:
                nxt = []
                for b in chain:
                    g_re, g_im = grads[b]
                    if layer:
                        w_re, w_im = saved[layer - 1, b, 0], saved[layer - 1, b, 1]
                        o_re, o_im = cut(layer, b, 0), cut(layer, b, 1)
                        nxt.append((o_re * g_re + o_im * g_im, o_re * g_im - o_im * g_re))
                    else:
                        w_re, w_im = probe_ref[0], probe_ref[1]
                    terms = (w_re * g_re + w_im * g_im, w_re * g_im - w_im * g_re)
                    for part in range(2):
                        moved = pltpu.roll(terms[part], forth[b], 1)
                        spot = pl.ds(top[b], patch)
                        acc[part, layer, 0, spot, :] += jnp.where(inside[b], moved, 0.0)
                        acc[part, layer, 1, spot, :] += jnp.where(inside[b], 0.0, moved)
                if layer:
                    for b, grad in zip(chain, backward_two_sided(kern_left[...], kern_right[...], nxt)):
                        grads[b] = grad

    rounds = (mine + 1) // BATCH
    rest = mine - rounds * BATCH
    most = jnp.where(rest > BATCH // 4, BATCH // 2, 0)

    def full(step, carry):
        group(step * BATCH, BATCH)
        return carry

    lax.fori_loop(0, rounds, full, 0)

    @pl.when(most > 0)
    def _():
        group(rounds * BATCH, BATCH // 2)

    @pl.when(rest > most)
    def _():
        group(rounds * BATCH + most, BATCH // 4)

    stores = []
    for result, spot in zip((near_keep, near_give, far_keep, far_give), spots):
        for part in range(2):
            for half in range(parts):
                stores.append(
                    pltpu.make_async_copy(
                        acc.at[part, :, half, pl.ds(spot * shard, shard), :],
                        result.at[part, :, :, pl.ds(half * patch, patch)],
                        out_sem.at[len(stores)],
                    )
                )
    for store in stores:
        store.start()
    for store in stores:
        store.wait()


def neighbours():
    tile, pos = lax.axis_index("tile"), lax.axis_index("pos")
    tiles = lax.axis_size("tile")
    sibling = (tile, pos + 1 - 2 * (pos % 2))
    across = (tile, (pos + 2) % 4)
    lower, upper = ((tile + tiles - 1) % tiles, pos), ((tile + 1) % tiles, pos)
    outer = pos < 2
    has_down = jnp.logical_and(outer, tile > 0)
    has_up = jnp.logical_and(outer, tile < tiles - 1)
    return sibling, across, lower, upper, outer, has_down, has_up


def greet(sibling, across, lower, upper, has_down, has_up):
    barrier = pltpu.get_barrier_semaphore()
    mesh_ids = pl.DeviceIdType.MESH
    pl.semaphore_signal(barrier, inc=1, device_id=sibling, device_id_type=mesh_ids)
    pl.semaphore_signal(barrier, inc=1, device_id=across, device_id_type=mesh_ids)

    @pl.when(has_down)
    def _():
        pl.semaphore_signal(barrier, inc=1, device_id=lower, device_id_type=mesh_ids)

    @pl.when(has_up)
    def _():
        pl.semaphore_signal(barrier, inc=1, device_id=upper, device_id_type=mesh_ids)

    pl.semaphore_wait(barrier, 2 + has_down.astype(jnp.int32) + has_up.astype(jnp.int32))


def remote(source, target, send, receive, device):
    return pltpu.make_async_remote_copy(
        src_ref=source, dst_ref=target, send_sem=send, recv_sem=receive,
        device_id=device, device_id_type=pl.DeviceIdType.MESH,
    )


def gather_kernel(
    re_ref, im_ref, near, nearsib, far, farsib,
    near_send, near_recv, far_send, far_recv, pass_send, pass_recv, fpass_send, fpass_recv,
):
    sibling, across, lower, upper, outer, has_down, has_up = neighbours()
    slices = re_ref.shape[0]
    fields = (re_ref, im_ref)
    chunks = list(enumerate((part, layer) for layer in range(slices) for part in range(2)))
    over = [remote(fields[p].at[s], near.at[p, s], near_send.at[k], near_recv.at[k], across) for k, (p, s) in chunks]
    down = [remote(fields[p].at[s], far.at[p, s], far_send.at[k], far_recv.at[k], lower) for k, (p, s) in chunks]
    over_pass = [remote(near.at[p, s], nearsib.at[p, s], pass_send.at[k], pass_recv.at[k], sibling) for k, (p, s) in chunks]
    down_pass = [remote(far.at[p, s], farsib.at[p, s], fpass_send.at[k], fpass_recv.at[k], sibling) for k, (p, s) in chunks]
    own_pass = [remote(fields[p].at[s], farsib.at[p, s], fpass_send.at[k], fpass_recv.at[k], sibling) for k, (p, s) in chunks]
    greet(sibling, across, lower, upper, has_down, has_up)

    @pl.when(has_down)
    def _():
        for one, other in zip(over, down):
            other.start()
            one.start()

    @pl.when(jnp.logical_not(has_down))
    def _():
        for one in over:
            one.start()

    @pl.when(jnp.logical_not(outer))
    def _():
        for copy in own_pass:
            copy.start()

    for k, _ in chunks:
        over[k].wait_recv()
        over_pass[k].start()

        @pl.when(has_up)
        def _():
            down[k].wait_recv()
            down_pass[k].start()

    @pl.when(has_up)
    def _():
        for copy in down_pass:
            copy.wait()

    @pl.when(jnp.logical_not(outer))
    def _():
        for copy in own_pass:
            copy.wait()

    for k, _ in chunks:
        over_pass[k].wait()
        over[k].wait_send()

    @pl.when(has_down)
    def _():
        for copy in down:
            copy.wait_send()


def scatter_kernel(
    near_keep, near_give, far_keep, far_give, from_near, from_far,
    near_kept, near_got, near_sum, far_kept, far_got, far_sum,
    nk_sem, fk_sem, ng_send, ng_recv, fg_send, fg_recv, near_send, near_recv, far_send, far_recv,
):
    sibling, across, lower, upper, outer, has_down, has_up = neighbours()
    slices = near_keep.shape[1]
    chunks = list(enumerate((part, layer) for layer in range(slices) for part in range(2)))
    near_loads = [pltpu.make_async_copy(near_keep.at[p, s], near_kept.at[p, s], nk_sem.at[k]) for k, (p, s) in chunks]
    far_loads = [pltpu.make_async_copy(far_keep.at[p, s], far_kept.at[p, s], fk_sem.at[k]) for k, (p, s) in chunks]
    near_gifts = [remote(near_give.at[p, s], near_got.at[p, s], ng_send.at[k], ng_recv.at[k], sibling) for k, (p, s) in chunks]
    far_gifts = [remote(far_give.at[p, s], far_got.at[p, s], fg_send.at[k], fg_recv.at[k], sibling) for k, (p, s) in chunks]
    over = [remote(near_sum.at[p, s], from_near.at[p, s], near_send.at[k], near_recv.at[k], across) for k, (p, s) in chunks]
    up = [remote(far_sum.at[p, s], from_far.at[p, s], far_send.at[k], far_recv.at[k], upper) for k, (p, s) in chunks]
    hold = [pltpu.make_async_copy(far_sum.at[p, s], from_far.at[p, s], far_send.at[k]) for k, (p, s) in chunks]
    for k, _ in chunks:
        near_loads[k].start()
        far_loads[k].start()
    greet(sibling, across, lower, upper, has_down, has_up)
    for k, _ in chunks:
        near_gifts[k].start()
        far_gifts[k].start()
    for k, (p, s) in chunks:
        near_loads[k].wait()
        near_gifts[k].wait_recv()
        near_sum[p, s] = near_kept[p, s] + near_got[p, s]
        over[k].start()
        far_loads[k].wait()
        far_gifts[k].wait_recv()
        far_sum[p, s] = far_kept[p, s] + far_got[p, s]

        @pl.when(has_up)
        def _():
            up[k].start()

        @pl.when(jnp.logical_not(outer))
        def _():
            hold[k].start()

    for k, _ in chunks:
        near_gifts[k].wait_send()
        far_gifts[k].wait_send()
        over[k].wait()

    @pl.when(jnp.logical_not(outer))
    def _():
        for copy in hold:
            copy.wait()

    @pl.when(has_up)
    def _():
        for copy in up:
            copy.wait_send()

    @pl.when(has_down)
    def _():
        for copy in up:
            copy.wait_recv()


def local(obj_real, obj_imag, probe, fresnel_phase, row_offset, col_offset, live_count, measured):
    slices, shard, width = obj_real.shape
    patch = probe.shape[-1]
    parts = width // patch
    taps = fresnel_phase.shape[0]
    chunks = 2 * slices
    assert lax.axis_size("pos") == 4 and 2 * shard == patch and parts == 2
    block = jax.ShapeDtypeStruct((2, slices, shard, width), jnp.float32)
    smem = pl.BlockSpec(memory_space=pltpu.SMEM)
    vmem = pl.BlockSpec(memory_space=pltpu.VMEM)
    anywhere = pl.BlockSpec(memory_space=pl.ANY)
    dma = pltpu.SemaphoreType.DMA
    near, nearsib, far, farsib = pl.pallas_call(
        gather_kernel,
        out_shape=[block] * 4,
        in_specs=[anywhere] * 2,
        out_specs=[anywhere] * 4,
        scratch_shapes=[dma((chunks,))] * 8,
        compiler_params=pltpu.CompilerParams(
            collective_id=0, has_side_effects=True, vmem_limit_bytes=VMEM_BYTES
        ),
        name="gather_rows",
    )(obj_real, obj_imag)
    phase = fresnel_phase.reshape(1, taps)
    dft_left, dft_right = dft_tables(patch)
    parts_of_sum = pl.pallas_call(
        functools.partial(compute_kernel, taps),
        out_shape=[block] * 4,
        in_specs=[smem] * 3 + [vmem] * 4 + [anywhere] * 7,
        out_specs=[anywhere] * 4,
        scratch_shapes=[
            pltpu.VMEM((2, slices, parts, 4 * shard, patch), jnp.float32),
            pltpu.VMEM((2, slices, parts, 4 * shard, patch), jnp.float32),
            pltpu.VMEM((measured.shape[0] // 2,) + measured.shape[1:], measured.dtype),
            pltpu.VMEM((2 * patch, 2 * patch), jnp.bfloat16),
            pltpu.VMEM((2 * patch, 2 * patch), jnp.bfloat16),
            pltpu.VMEM((slices - 1, BATCH, 2, patch, patch), jnp.float32),
            pltpu.VMEM((1, patch), jnp.float32),
            pltpu.SMEM((row_offset.shape[0] + 8,), jnp.int32),
            pltpu.SemaphoreType.DMA((8 * parts,)),
            pltpu.SemaphoreType.DMA((measured.shape[0] // 2,)),
            pltpu.SemaphoreType.DMA((8 * parts,)),
        ],
        compiler_params=pltpu.CompilerParams(vmem_limit_bytes=VMEM_BYTES),
        name="patch_gradients",
    )(
        row_offset, col_offset, live_count, phase, dft_left, dft_right, probe,
        obj_real, obj_imag, near, nearsib, far, farsib, measured,
    )
    from_near, from_far = pl.pallas_call(
        scatter_kernel,
        out_shape=[block] * 2,
        in_specs=[anywhere] * 4,
        out_specs=[anywhere] * 2,
        scratch_shapes=[pltpu.VMEM(block.shape, jnp.float32)] * 6 + [dma((chunks,))] * 10,
        compiler_params=pltpu.CompilerParams(
            collective_id=1, has_side_effects=True, vmem_limit_bytes=VMEM_BYTES
        ),
        name="scatter_rows",
    )(*parts_of_sum)
    alone = jnp.logical_and(lax.axis_index("tile") == 0, lax.axis_index("pos") < 2)
    return tuple(from_near[p] + jnp.where(alone, 0.0, from_far[p]) for p in range(2))


def solution(mesh):
    in_specs = (
        P(None, ("tile", "pos"), None),
        P(None, ("tile", "pos"), None),
        P(),
        P(),
        P("tile"),
        P("tile"),
        P("tile"),
        P("tile", None, None),
    )
    out_specs = (P(None, ("tile", "pos"), None), P(None, ("tile", "pos"), None))
    return jax.shard_map(local, mesh=mesh, in_specs=in_specs, out_specs=out_specs, check_vma=False)
```

```python
import functools

import jax
import jax.numpy as jnp
import ml_dtypes
import numpy as np
from jax import lax
from jax.experimental import pallas as pl
from jax.experimental.pallas import tpu as pltpu
from jax.sharding import PartitionSpec as P

AMP_FLOOR = 0.25
BATCH = 4
CHAIN = 2
VMEM_BYTES = 60 * 1024 * 1024


def dft_tables(patch):
    grid = np.arange(patch)
    product = (grid[:, None] * grid[None, :] % patch).astype(np.float32)
    angle = np.float32(2.0 * np.pi / patch) * product
    norm = np.float32(1.0) / np.sqrt(np.float32(patch))
    real = (np.cos(angle) * norm).astype(ml_dtypes.bfloat16)
    imag = (-np.sin(angle) * norm).astype(ml_dtypes.bfloat16)
    left = np.block([[real, -imag], [imag, real]])
    right = np.block([[real.T, imag.T], [-imag.T, real.T]])
    return jnp.asarray(left), jnp.asarray(right)


def dot(left, right):
    return jnp.dot(left, right, preferred_element_type=jnp.float32)


def stack_rows(pairs):
    return jnp.concatenate([jnp.concatenate(pair, axis=0) for pair in pairs], axis=1)


def stack_cols(pairs):
    return jnp.concatenate([jnp.concatenate(pair, axis=1) for pair in pairs], axis=0)


def split_rows(array, patch):
    count = array.shape[1] // patch
    return [
        (array[:patch, b * patch : (b + 1) * patch], array[patch:, b * patch : (b + 1) * patch])
        for b in range(count)
    ]


def split_cols(array, patch):
    count = array.shape[0] // patch
    return [
        (array[b * patch : (b + 1) * patch, :patch], array[b * patch : (b + 1) * patch, patch:])
        for b in range(count)
    ]


def halves(pairs):
    return [(a.astype(jnp.bfloat16), b.astype(jnp.bfloat16)) for a, b in pairs]


def forward_two_sided(left, right, pairs):
    patch = pairs[0][0].shape[0]
    inner = split_rows(dot(left, stack_rows(halves(pairs))), patch)
    return split_cols(dot(stack_cols(halves(inner)), right), patch)


def backward_two_sided(left, right, pairs):
    patch = pairs[0][0].shape[0]
    inner = split_cols(dot(stack_cols(halves(pairs)), left), patch)
    return split_rows(dot(right, stack_rows(halves(inner))), patch)


def compute_kernel(
    taps, rows_ref, cols_ref, live_ref, phase_ref, dft_left, dft_right, probe_ref,
    own_re, own_im, near_ref, nearsib_ref, far_ref, farsib_ref, measured_ref,
    near_keep, near_give, far_keep, far_give,
    window, acc, target, kern_left, kern_right, saved, phases, listed, in_sem, target_sem, out_sem,
):
    slices, shard, width = own_re.shape
    patch = probe_ref.shape[-1]
    slots = rows_ref.shape[0]
    parts = width // patch
    member = lax.axis_index("pos")
    parity = member % 2

    def get_target(item, slot):
        return pltpu.make_async_copy(measured_ref.at[slot], target.at[item], target_sem.at[item])

    outer = member < 2
    ahead = jnp.logical_and(outer, lax.axis_index("tile") + 1 < lax.axis_size("tile"))
    base = jnp.where(outer, 2 * shard, 0)
    spots = (parity, 1 - parity, 2 + parity, 3 - parity)

    def loads_of(real, imag, place):
        return [
            pltpu.make_async_copy(
                source.at[:, :, pl.ds(half * patch, patch)],
                window.at[part, :, half, pl.ds(spots[place] * shard, shard), :],
                in_sem.at[(place * 2 + part) * parts + half],
            )
            for part, source in enumerate((real, imag))
            for half in range(parts)
        ]

    near_loads = loads_of(near_ref.at[0], near_ref.at[1], 0)
    near_loads += loads_of(nearsib_ref.at[0], nearsib_ref.at[1], 1)
    own_loads = loads_of(own_re, own_im, 2)
    far_loads = loads_of(far_ref.at[0], far_ref.at[1], 2)
    farsib_loads = loads_of(farsib_ref.at[0], farsib_ref.at[1], 3)
    for load in near_loads:
        load.start()

    @pl.when(jnp.logical_not(outer))
    def _():
        for load in own_loads + farsib_loads:
            load.start()

    @pl.when(ahead)
    def _():
        for load in far_loads + farsib_loads:
            load.start()

    @pl.when(jnp.logical_and(outer, jnp.logical_not(ahead)))
    def _():
        window[:, :, :, 2 * shard :, :] = jnp.zeros(
            window.shape[:3] + (2 * shard, patch), window.dtype
        )

    def pick(slot, count):
        ok = jnp.logical_and(slot < live_ref[0], (rows_ref[slot] >= 2 * shard) == outer)
        take = jnp.logical_and(ok, count % 2 == parity)
        listed[jnp.where(take, count // 2, slots)] = slot
        return count + ok.astype(jnp.int32)

    total = lax.fori_loop(0, slots, pick, jnp.int32(0))
    mine = (total + 1 - parity) // 2

    def fetch(item, carry):
        get_target(item, listed[item]).start()
        return carry

    lax.fori_loop(0, mine, fetch, 0)

    row = lax.broadcasted_iota(jnp.int32, (patch, patch), 0)
    col = lax.broadcasted_iota(jnp.int32, (patch, patch), 1)
    band = jnp.logical_and(col - row + taps // 2 >= 0, col - row + taps // 2 < taps)
    scale = 1.0 / jnp.sqrt(jnp.float32(taps))

    def toeplitz(values):
        wide = jnp.broadcast_to(values, (patch, patch))
        moved = pltpu.roll(wide, patch - taps // 2, 1, stride=1, stride_axis=0)
        return jnp.where(band, moved, 0.0)

    phases[...] = jnp.zeros_like(phases)
    phases[:, :taps] = phase_ref[...]
    kern_re = toeplitz(jnp.cos(phases[...]) * scale)
    kern_im = toeplitz(jnp.sin(phases[...]) * scale)
    kern_left[...] = stack_rows(halves([(kern_re, kern_im), (-kern_im, kern_re)]))
    kern_re_t, kern_im_t = kern_re.T, kern_im.T
    kern_right[...] = stack_rows(halves([(kern_re_t, -kern_im_t), (kern_im_t, kern_re_t)]))
    acc[...] = jnp.zeros_like(acc)
    for load in near_loads:
        load.wait()

    @pl.when(jnp.logical_or(jnp.logical_not(outer), ahead))
    def _():
        for load in far_loads + farsib_loads:
            load.wait()

    def group(first, size):
        def arrive(item, carry):
            get_target(item, listed[item]).wait()
            return carry

        lax.fori_loop(first, jnp.minimum(first + size, mine), arrive, 0)
        every = range(size)
        chains = [list(every)[c : c + CHAIN] for c in range(0, size, CHAIN)]
        item = [jnp.minimum(first + b, mine - 1) for b in every]
        index = [listed[i] for i in item]
        weight = [(first + b < mine).astype(jnp.float32) for b in every]
        top = [rows_ref[i] - base for i in index]
        left = [cols_ref[i] for i in index]
        back = [(patch - x) % patch for x in left]
        forth = [x % patch for x in left]
        inside = [col >= x for x in left]

        def cut(layer, b, part):
            a0 = window[part, layer, 0, pl.ds(top[b], patch), :]
            a1 = window[part, layer, 1, pl.ds(top[b], patch), :]
            return pltpu.roll(jnp.where(inside[b], a0, a1), back[b], 1)

        waves = [(probe_ref[0], probe_ref[1]) for _ in every]
        for layer in range(slices):
            for chain in chains:
                nxt = []
                for b in chain:
                    o_re, o_im = cut(layer, b, 0), cut(layer, b, 1)
                    w_re, w_im = waves[b]
                    if layer:
                        saved[layer - 1, b, 0] = w_re
                        saved[layer - 1, b, 1] = w_im
                    nxt.append((w_re * o_re - w_im * o_im, w_re * o_im + w_im * o_re))
                last = layer + 1 == slices
                lhs, rhs = (dft_left, dft_right) if last else (kern_left, kern_right)
                for b, wave in zip(chain, forward_two_sided(lhs[...], rhs[...], nxt)):
                    waves[b] = wave
        grads = list(waves)
        for chain in chains:
            nxt = []
            for b in chain:
                f_re, f_im = waves[b]
                inverse = lax.rsqrt(f_re * f_re + f_im * f_im + AMP_FLOOR)
                t = target[item[b]].astype(jnp.float32)
                ratio = weight[b] * (1.0 - t * inverse)
                nxt.append((f_re * ratio, f_im * ratio))
            for b, grad in zip(chain, backward_two_sided(dft_left[...], dft_right[...], nxt)):
                grads[b] = grad
        for layer in reversed(range(slices)):
            for chain in chains:
                nxt = []
                for b in chain:
                    g_re, g_im = grads[b]
                    if layer:
                        w_re, w_im = saved[layer - 1, b, 0], saved[layer - 1, b, 1]
                        o_re, o_im = cut(layer, b, 0), cut(layer, b, 1)
                        nxt.append((o_re * g_re + o_im * g_im, o_re * g_im - o_im * g_re))
                    else:
                        w_re, w_im = probe_ref[0], probe_ref[1]
                    terms = (w_re * g_re + w_im * g_im, w_re * g_im - w_im * g_re)
                    for part in range(2):
                        moved = pltpu.roll(terms[part], forth[b], 1)
                        spot = pl.ds(top[b], patch)
                        acc[part, layer, 0, spot, :] += jnp.where(inside[b], moved, 0.0)
                        acc[part, layer, 1, spot, :] += jnp.where(inside[b], 0.0, moved)
                if layer:
                    for b, grad in zip(chain, backward_two_sided(kern_left[...], kern_right[...], nxt)):
                        grads[b] = grad

    rounds = (mine + 1) // BATCH
    rest = mine - rounds * BATCH
    most = jnp.where(rest > BATCH // 4, BATCH // 2, 0)

    def full(step, carry):
        group(step * BATCH, BATCH)
        return carry

    lax.fori_loop(0, rounds, full, 0)

    @pl.when(most > 0)
    def _():
        group(rounds * BATCH, BATCH // 2)

    @pl.when(rest > most)
    def _():
        group(rounds * BATCH + most, BATCH // 4)

    stores = []
    for result, spot in zip((near_keep, near_give, far_keep, far_give), spots):
        for part in range(2):
            for half in range(parts):
                stores.append(
                    pltpu.make_async_copy(
                        acc.at[part, :, half, pl.ds(spot * shard, shard), :],
                        result.at[part, :, :, pl.ds(half * patch, patch)],
                        out_sem.at[len(stores)],
                    )
                )
    for store in stores:
        store.start()
    for store in stores:
        store.wait()


def neighbours():
    tile, pos = lax.axis_index("tile"), lax.axis_index("pos")
    tiles = lax.axis_size("tile")
    sibling = (tile, pos + 1 - 2 * (pos % 2))
    across = (tile, (pos + 2) % 4)
    lower, upper = ((tile + tiles - 1) % tiles, pos), ((tile + 1) % tiles, pos)
    outer = pos < 2
    has_down = jnp.logical_and(outer, tile > 0)
    has_up = jnp.logical_and(outer, tile < tiles - 1)
    return sibling, across, lower, upper, outer, has_down, has_up


def greet(sibling, across, lower, upper, has_down, has_up):
    barrier = pltpu.get_barrier_semaphore()
    mesh_ids = pl.DeviceIdType.MESH
    pl.semaphore_signal(barrier, inc=1, device_id=sibling, device_id_type=mesh_ids)
    pl.semaphore_signal(barrier, inc=1, device_id=across, device_id_type=mesh_ids)

    @pl.when(has_down)
    def _():
        pl.semaphore_signal(barrier, inc=1, device_id=lower, device_id_type=mesh_ids)

    @pl.when(has_up)
    def _():
        pl.semaphore_signal(barrier, inc=1, device_id=upper, device_id_type=mesh_ids)

    pl.semaphore_wait(barrier, 2 + has_down.astype(jnp.int32) + has_up.astype(jnp.int32))


def remote(source, target, send, receive, device):
    return pltpu.make_async_remote_copy(
        src_ref=source, dst_ref=target, send_sem=send, recv_sem=receive,
        device_id=device, device_id_type=pl.DeviceIdType.MESH,
    )


def gather_kernel(
    re_ref, im_ref, near, nearsib, far, farsib,
    near_send, near_recv, far_send, far_recv, pass_send, pass_recv, fpass_send, fpass_recv,
):
    sibling, across, lower, upper, outer, has_down, has_up = neighbours()
    slices = re_ref.shape[0]
    fields = (re_ref, im_ref)
    chunks = list(enumerate((part, layer) for layer in range(slices) for part in range(2)))
    over = [remote(fields[p].at[s], near.at[p, s], near_send.at[k], near_recv.at[k], across) for k, (p, s) in chunks]
    down = [remote(fields[p].at[s], far.at[p, s], far_send.at[k], far_recv.at[k], lower) for k, (p, s) in chunks]
    over_pass = [remote(near.at[p, s], nearsib.at[p, s], pass_send.at[k], pass_recv.at[k], sibling) for k, (p, s) in chunks]
    down_pass = [remote(far.at[p, s], farsib.at[p, s], fpass_send.at[k], fpass_recv.at[k], sibling) for k, (p, s) in chunks]
    own_pass = [remote(fields[p].at[s], farsib.at[p, s], fpass_send.at[k], fpass_recv.at[k], sibling) for k, (p, s) in chunks]
    greet(sibling, across, lower, upper, has_down, has_up)

    @pl.when(has_down)
    def _():
        for one, other in zip(over, down):
            other.start()
            one.start()

    @pl.when(jnp.logical_not(has_down))
    def _():
        for one in over:
            one.start()

    @pl.when(jnp.logical_not(outer))
    def _():
        for copy in own_pass:
            copy.start()

    for k, _ in chunks:
        over[k].wait_recv()
        over_pass[k].start()

        @pl.when(has_up)
        def _():
            down[k].wait_recv()
            down_pass[k].start()

    @pl.when(has_up)
    def _():
        for copy in down_pass:
            copy.wait()

    @pl.when(jnp.logical_not(outer))
    def _():
        for copy in own_pass:
            copy.wait()

    for k, _ in chunks:
        over_pass[k].wait()
        over[k].wait_send()

    @pl.when(has_down)
    def _():
        for copy in down:
            copy.wait_send()


def scatter_kernel(
    near_keep, near_give, far_keep, far_give, from_near, from_far,
    near_kept, near_got, near_sum, far_kept, far_got, far_sum,
    nk_sem, fk_sem, ng_send, ng_recv, fg_send, fg_recv, near_send, near_recv, far_send, far_recv,
):
    sibling, across, lower, upper, outer, has_down, has_up = neighbours()
    slices = near_keep.shape[1]
    chunks = list(enumerate((part, layer) for layer in range(slices) for part in range(2)))
    near_loads = [pltpu.make_async_copy(near_keep.at[p, s], near_kept.at[p, s], nk_sem.at[k]) for k, (p, s) in chunks]
    far_loads = [pltpu.make_async_copy(far_keep.at[p, s], far_kept.at[p, s], fk_sem.at[k]) for k, (p, s) in chunks]
    near_gifts = [remote(near_give.at[p, s], near_got.at[p, s], ng_send.at[k], ng_recv.at[k], sibling) for k, (p, s) in chunks]
    far_gifts = [remote(far_give.at[p, s], far_got.at[p, s], fg_send.at[k], fg_recv.at[k], sibling) for k, (p, s) in chunks]
    over = [remote(near_sum.at[p, s], from_near.at[p, s], near_send.at[k], near_recv.at[k], across) for k, (p, s) in chunks]
    up = [remote(far_sum.at[p, s], from_far.at[p, s], far_send.at[k], far_recv.at[k], upper) for k, (p, s) in chunks]
    blank = [pltpu.make_async_copy(near_kept.at[p, s], from_far.at[p, s], nk_sem.at[k]) for k, (p, s) in chunks]
    hold = [pltpu.make_async_copy(far_sum.at[p, s], from_far.at[p, s], far_send.at[k]) for k, (p, s) in chunks]
    for k, _ in chunks:
        near_loads[k].start()
        far_loads[k].start()
    greet(sibling, across, lower, upper, has_down, has_up)
    for k, _ in chunks:
        near_gifts[k].start()
        far_gifts[k].start()
    for k, (p, s) in chunks:
        near_loads[k].wait()
        near_gifts[k].wait_recv()
        near_sum[p, s] = near_kept[p, s] + near_got[p, s]
        over[k].start()
        far_loads[k].wait()
        far_gifts[k].wait_recv()
        far_sum[p, s] = far_kept[p, s] + far_got[p, s]

        @pl.when(has_up)
        def _():
            up[k].start()

        @pl.when(jnp.logical_not(outer))
        def _():
            hold[k].start()

    @pl.when(jnp.logical_and(outer, jnp.logical_not(has_down)))
    def _():
        near_kept[...] = jnp.zeros_like(near_kept)
        for copy in blank:
            copy.start()
        for copy in blank:
            copy.wait()

    for k, _ in chunks:
        near_gifts[k].wait_send()
        far_gifts[k].wait_send()
        over[k].wait()

    @pl.when(jnp.logical_not(outer))
    def _():
        for copy in hold:
            copy.wait()

    @pl.when(has_up)
    def _():
        for copy in up:
            copy.wait_send()

    @pl.when(has_down)
    def _():
        for copy in up:
            copy.wait_recv()


def local(obj_real, obj_imag, probe, fresnel_phase, row_offset, col_offset, live_count, measured):
    slices, shard, width = obj_real.shape
    patch = probe.shape[-1]
    parts = width // patch
    taps = fresnel_phase.shape[0]
    chunks = 2 * slices
    assert lax.axis_size("pos") == 4 and 2 * shard == patch and parts == 2
    block = jax.ShapeDtypeStruct((2, slices, shard, width), jnp.float32)
    smem = pl.BlockSpec(memory_space=pltpu.SMEM)
    vmem = pl.BlockSpec(memory_space=pltpu.VMEM)
    anywhere = pl.BlockSpec(memory_space=pl.ANY)
    dma = pltpu.SemaphoreType.DMA
    near, nearsib, far, farsib = pl.pallas_call(
        gather_kernel,
        out_shape=[block] * 4,
        in_specs=[anywhere] * 2,
        out_specs=[anywhere] * 4,
        scratch_shapes=[dma((chunks,))] * 8,
        compiler_params=pltpu.CompilerParams(
            collective_id=0, has_side_effects=True, vmem_limit_bytes=VMEM_BYTES
        ),
        name="gather_rows",
    )(obj_real, obj_imag)
    phase = fresnel_phase.reshape(1, taps)
    dft_left, dft_right = dft_tables(patch)
    parts_of_sum = pl.pallas_call(
        functools.partial(compute_kernel, taps),
        out_shape=[block] * 4,
        in_specs=[smem] * 3 + [vmem] * 4 + [anywhere] * 7,
        out_specs=[anywhere] * 4,
        scratch_shapes=[
            pltpu.VMEM((2, slices, parts, 4 * shard, patch), jnp.float32),
            pltpu.VMEM((2, slices, parts, 4 * shard, patch), jnp.float32),
            pltpu.VMEM((measured.shape[0] // 2,) + measured.shape[1:], measured.dtype),
            pltpu.VMEM((2 * patch, 2 * patch), jnp.bfloat16),
            pltpu.VMEM((2 * patch, 2 * patch), jnp.bfloat16),
            pltpu.VMEM((slices - 1, BATCH, 2, patch, patch), jnp.float32),
            pltpu.VMEM((1, patch), jnp.float32),
            pltpu.SMEM((row_offset.shape[0] + 8,), jnp.int32),
            pltpu.SemaphoreType.DMA((8 * parts,)),
            pltpu.SemaphoreType.DMA((measured.shape[0] // 2,)),
            pltpu.SemaphoreType.DMA((8 * parts,)),
        ],
        compiler_params=pltpu.CompilerParams(vmem_limit_bytes=VMEM_BYTES),
        name="patch_gradients",
    )(
        row_offset, col_offset, live_count, phase, dft_left, dft_right, probe,
        obj_real, obj_imag, near, nearsib, far, farsib, measured,
    )
    from_near, from_far = pl.pallas_call(
        scatter_kernel,
        out_shape=[block] * 2,
        in_specs=[anywhere] * 4,
        out_specs=[anywhere] * 2,
        scratch_shapes=[pltpu.VMEM(block.shape, jnp.float32)] * 6 + [dma((chunks,))] * 10,
        compiler_params=pltpu.CompilerParams(
            collective_id=1, has_side_effects=True, vmem_limit_bytes=VMEM_BYTES
        ),
        name="scatter_rows",
    )(*parts_of_sum)
    return tuple(from_near[p] + from_far[p] for p in range(2))


def solution(mesh):
    in_specs = (
        P(None, ("tile", "pos"), None),
        P(None, ("tile", "pos"), None),
        P(),
        P(),
        P("tile"),
        P("tile"),
        P("tile"),
        P("tile", None, None),
    )
    out_specs = (P(None, ("tile", "pos"), None), P(None, ("tile", "pos"), None))
    return jax.shard_map(local, mesh=mesh, in_specs=in_specs, out_specs=out_specs, check_vma=False)
```
